128 devices in a mesh: grp: 8 (over z_hi, y), seq: 16 (over x, z_lo, core).
Axes of the slice: x: 4, y: 4, z: 4 (z_hi: 2, z_lo: 2; z = z_hi * 2 + z_lo), core: 2. Of those that a mesh axis runs over, the one named last changes fastest.
Arguments:
- queries: bfloat16 [128, 1024, 1024], P(('grp', 'seq')), may hold values from -12 to 12
- key_vectors: bfloat16 [128, 1024, 1024], P(('grp', 'seq')), may hold values from -6 to 6
- value_vectors: bfloat16 [128, 1024, 1024], P(('grp', 'seq')), may hold values from -6 to 6
- out_cotangent: bfloat16 [128, 1024, 1024], P(('grp', 'seq')), may hold values from -6 to 6
Outputs:
- attended: bfloat16 [128, 1024, 1024], P(('grp', 'seq'))
- query_grad: bfloat16 [128, 1024, 1024], P(('grp', 'seq'))
- key_grad: bfloat16 [128, 1024, 1024], P(('grp', 'seq'))
- value_grad: bfloat16 [128, 1024, 1024], P(('grp', 'seq'))
The draws below stay inside these ranges and needn't reach their ends.
All inputs are finite; a program needn't handle non-finite values.
Results may differ from the reference program's by a relative error of at most 0.028.
Values may be sent and summed in bfloat16 or wider, within the bound.
No kernel may reach another device: no remote copies, remote signals or barrier semaphores. Data moves between devices by JAX's collectives and lax.ppermute only.
A program may use at most 192 MiB of HBM per device.

```python
import jax
import jax.numpy as jnp
from jax import lax

HEADS = 8
HDIM = 128
STRIDE = 1024
ROWS = 128
HD = 1024


def draw_queries(key, part):
    key = jax.random.fold_in(key, 1)
    sample_count = ROWS * STRIDE
    feature_width = HEADS * HDIM
    base = jnp.clip(jax.random.normal(key, (sample_count, feature_width), jnp.float32) * 2.5, -12.0, 12.0)
    return base.reshape(ROWS, STRIDE, feature_width).astype(jnp.bfloat16)


def draw_key_vectors(key, part):
    key = jax.random.fold_in(key, 2)
    sample_count = ROWS * STRIDE
    feature_width = HEADS * HDIM
    base = jnp.clip(jax.random.normal(key, (sample_count, feature_width), jnp.float32), -6.0, 6.0)
    return base.reshape(ROWS, STRIDE, feature_width).astype(jnp.bfloat16)


def levels(stream_key, extent, cuts, least, top_value):
    def one(axis_at, blocks):
        heights = jax.random.uniform(jax.random.fold_in(jax.random.fold_in(stream_key, 6), axis_at), (blocks,), jnp.float32, least / len(cuts), top_value / len(cuts))
        return jnp.repeat(jnp.exp(heights), extent[axis_at] // blocks).reshape((-1,) + (1,) * (len(extent) - axis_at - 1))

    gain = one(*cuts[0])
    for cut in cuts[1:]:
        gain = gain * one(*cut)
    return gain


def gaussian(stream_key, extent, deviation, most, split=(), kind=jnp.bfloat16):
    drawn = jax.random.normal(stream_key, extent, jnp.float32) * deviation
    if len(split) > 0:
        drawn = levels(stream_key, extent, split, -0.22, 0.18) * drawn
    return jnp.clip(drawn, min=-most, max=most).astype(kind)


def setup_inputs(seed: int = 0) -> dict:
    key_list = jax.random.split(jax.random.key(seed), 5)
    return {
        "queries": draw_queries(jax.random.fold_in(key_list[4], 71), 0),
        "key_vectors": draw_key_vectors(jax.random.fold_in(key_list[4], 71), 0),
        "value_vectors": gaussian(key_list[2], (ROWS, STRIDE, HD), 1.0, 6.0, ((0, 128),)),
        "out_cotangent": gaussian(key_list[3], (ROWS, STRIDE, HD), 1.0, 6.0, ((0, 128),)),
    }


NEG = -1e30


def rounded(array):
    return lax.optimization_barrier(array.astype(jnp.bfloat16)).astype(jnp.float32)


def attend_block(query_blk, key_win, value_win, grad_blk, allowed, scaling):
    query_wide = query_blk.astype(jnp.float32)
    key_wide = key_win.astype(jnp.float32)
    value_wide = value_win.astype(jnp.float32)
    grad_wide = grad_blk.astype(jnp.float32)
    scores = jnp.einsum("bnd,wnd->nbw", query_wide, key_wide) * scaling
    scores = jnp.where(allowed[None], scores, NEG)
    peak_score = jnp.max(scores, axis=-1)
    exp_scores = jnp.where(allowed[None], jnp.exp(scores - peak_score[..., None]), 0.0)
    denominator = jnp.sum(exp_scores, axis=-1)
    summed = jnp.einsum("nbw,wnd->bnd", rounded(exp_scores), value_wide)
    attended = (summed / jnp.transpose(denominator)[..., None]).astype(jnp.bfloat16)
    log_total = peak_score + jnp.log(denominator)
    probability = jnp.where(allowed[None], jnp.exp(scores - log_total[..., None]), 0.0)
    row_dot = jnp.sum(grad_wide * attended.astype(jnp.float32), axis=-1)
    dprob = jnp.einsum("bnd,wnd->nbw", grad_wide, value_wide)
    dscore = rounded(probability * (dprob - jnp.transpose(row_dot)[..., None]))
    query_grad = jnp.einsum("nbw,wnd->bnd", dscore, key_wide) * scaling
    key_grad = jnp.einsum("nbw,bnd->wnd", dscore, query_wide) * scaling
    value_grad = jnp.einsum("nbw,bnd->wnd", rounded(probability), grad_wide)
    return attended, query_grad, key_grad, value_grad


def reference(queries, key_vectors, value_vectors, out_cotangent):
    row_count, stride_len, feature_width = queries.shape
    half_width = feature_width // 2
    head_half = HEADS // 2
    scaling = HDIM ** -0.5
    token_count = row_count * stride_len

    def row_part(array):
        return array[..., :half_width].reshape(token_count, head_half, HDIM)

    query_rows = row_part(queries)
    key_rows = row_part(key_vectors)
    value_rows = row_part(value_vectors)
    grad_rows = row_part(out_cotangent)
    padding = jnp.zeros((stride_len, head_half, HDIM), jnp.bfloat16)
    key_ext = jnp.concatenate([padding, key_rows], axis=0)
    value_ext = jnp.concatenate([padding, value_rows], axis=0)
    block_len = stride_len // 2
    window = stride_len + block_len
    local_query = jnp.arange(block_len, dtype=jnp.int32)[:, None]
    local_key = jnp.arange(window, dtype=jnp.int32)[None, :]
    in_band = (local_key > local_query) & (local_key <= local_query + stride_len)

    def step(sums_in, block_idx):
        key_acc, value_acc = sums_in
        offset = block_idx * block_len
        query_blk = lax.dynamic_slice_in_dim(query_rows, offset, block_len, 0)
        grad_blk = lax.dynamic_slice_in_dim(grad_rows, offset, block_len, 0)
        key_win = lax.dynamic_slice_in_dim(key_ext, offset, window, 0)
        value_win = lax.dynamic_slice_in_dim(value_ext, offset, window, 0)
        allowed = in_band & (local_key + offset >= stride_len)
        attended, query_grad, key_grad, value_grad = attend_block(query_blk, key_win, value_win, grad_blk, allowed, scaling)
        key_acc = lax.dynamic_update_slice_in_dim(key_acc, lax.dynamic_slice_in_dim(key_acc, offset, window, 0) + key_grad, offset, 0)
        value_acc = lax.dynamic_update_slice_in_dim(value_acc, lax.dynamic_slice_in_dim(value_acc, offset, window, 0) + value_grad, offset, 0)
        return (key_acc, value_acc), (attended, query_grad.astype(jnp.bfloat16))

    zeros_ext = jnp.zeros((token_count + stride_len, head_half, HDIM), jnp.float32)
    block_ids = jnp.arange(token_count // block_len, dtype=jnp.int32)
    (key_acc, value_acc), (row_out, row_qgrad) = lax.scan(step, (zeros_ext, zeros_ext), block_ids)

    per_group = 8
    group_count = stride_len // per_group

    def col_part(array):
        shaped = array[..., half_width:].reshape(row_count, group_count, per_group, head_half, HDIM)
        return jnp.moveaxis(shaped, 1, 0)

    causal = jnp.arange(row_count, dtype=jnp.int32)[None, :] <= jnp.arange(row_count, dtype=jnp.int32)[:, None]

    def one_column(query_col, key_col, value_col, grad_col):
        return attend_block(query_col, key_col, value_col, grad_col, causal, scaling)

    def column_group(pieces):
        return jax.vmap(one_column, in_axes=1, out_axes=1)(pieces[0], pieces[1], pieces[2], pieces[3])

    col_out, col_q, col_k, col_v = lax.map(column_group, (col_part(queries), col_part(key_vectors), col_part(value_vectors), col_part(out_cotangent)))

    def back(array):
        return jnp.moveaxis(array, 0, 1).reshape(row_count, stride_len, half_width)

    def rows_back(array):
        return array.reshape(row_count, stride_len, half_width)

    attended = jnp.concatenate([rows_back(row_out), back(col_out)], axis=-1)
    query_grad = jnp.concatenate([rows_back(row_qgrad), back(col_q).astype(jnp.bfloat16)], axis=-1)
    key_grad = jnp.concatenate([rows_back(key_acc[stride_len:].astype(jnp.bfloat16)), back(col_k).astype(jnp.bfloat16)], axis=-1)
    value_grad = jnp.concatenate([rows_back(value_acc[stride_len:].astype(jnp.bfloat16)), back(col_v).astype(jnp.bfloat16)], axis=-1)
    return attended, query_grad, key_grad, value_grad
```

```python
import functools
import math

import jax
import jax.numpy as jnp
from jax import lax
from jax.experimental import pallas as pl
from jax.experimental.pallas import tpu as pltpu
from jax.sharding import PartitionSpec as P

HEADS = 8
HDIM = 128
HALF = HEADS // 2
SCALING = HDIM ** (-0.5)
LOG2E = math.log2(math.e)
NEG = -1e30
AXES = ("grp", "seq")
F32 = jnp.float32
BF16 = jnp.bfloat16


def matmul(lhs, rhs):
    return jnp.dot(lhs, rhs, preferred_element_type=F32)


def matmul_nt(lhs, rhs):
    return lax.dot_general(lhs, rhs, (((1,), (1,)), ((), ())), preferred_element_type=F32)


def matmul_tn(lhs, rhs):
    return lax.dot_general(lhs, rhs, (((0,), (0,)), ((), ())), preferred_element_type=F32)


def params(mib):
    return pltpu.CompilerParams(
        dimension_semantics=("arbitrary",), vmem_limit_bytes=mib * 1024 * 1024
    )


def pack_kernel(q_ref, k_ref, v_ref, g_ref, out_ref):
    for at, ref in enumerate((q_ref, k_ref, v_ref, g_ref)):
        block = ref[0]
        out_ref[:, at] = block.reshape(out_ref.shape[0], out_ref.shape[2], block.shape[1])


def pack_columns(arrays, devices):
    _, stride_len, width = arrays[0].shape
    half = width // 2
    per = stride_len // devices
    step = 16
    return pl.pallas_call(
        pack_kernel,
        grid=(devices // step,),
        in_specs=[pl.BlockSpec((1, step * per, half), lambda i: (0, i, 1))] * 4,
        out_specs=pl.BlockSpec((step, 4, per, half), lambda i: (i, 0, 0, 0)),
        out_shape=jax.ShapeDtypeStruct((devices, 4, per, half), BF16),
        compiler_params=params(32),
        cost_estimate=pl.CostEstimate(
            flops=0, bytes_accessed=16 * stride_len * half, transcendentals=0
        ),
        name="pack_columns",
    )(*arrays)


def row_kernel(
    block,
    bias_ref,
    q_ref,
    k_ref,
    v_ref,
    g_ref,
    prior_ref,
    out_ref,
    dq_ref,
    dk_ref,
    dv_ref,
    dprior_ref,
    keys,
    values,
    keys_t,
    values_t,
    scores,
    dkeys,
    dvalues,
):
    length = q_ref.shape[1]
    window = length + block
    parts = window // block
    keys[:length] = prior_ref[0]
    keys[length:] = k_ref[0]
    values[:length] = prior_ref[1]
    values[length:] = v_ref[0]
    for at in range(0, 2 * length, block):
        rows = slice(at, at + block)
        keys_t[:, rows] = keys[rows].T
        values_t[:, rows] = values[rows].T
    dkeys[...] = jnp.zeros_like(dkeys)
    dvalues[...] = jnp.zeros_like(dvalues)
    bias = bias_ref[0]
    key_at = lax.broadcasted_iota(jnp.int32, (block, block), 0)
    query_at = lax.broadcasted_iota(jnp.int32, (block, block), 1)
    older = key_at > query_at
    for qi in range(length // block):
        here = slice(qi * block, (qi + 1) * block)
        query = q_ref[0, here]
        grad = g_ref[0, here]
        query_t = query.T
        grad_t = grad.T

        def rows_of(part):
            start = qi * block + part * block
            return slice(start, start + block)

        def is_prior(part):
            return (qi + part) * block < length

        peak = jnp.full((1, block), NEG, F32)
        for part in range(parts):
            score = matmul(keys[rows_of(part)], query_t)
            if part == 0:
                score = jnp.where(older, score, NEG)
            if part == parts - 1:
                score = jnp.where(older, NEG, score)
            top = jnp.max(score, axis=0, keepdims=True)
            if is_prior(part):
                top = top + bias
            peak = jnp.maximum(peak, top)
            scores[part * block : (part + 1) * block] = score
        factor = SCALING * LOG2E
        scaled_peak = peak * factor
        shifted_prior = (peak - bias) * factor
        total = jnp.zeros((1, block), F32)
        for part in range(parts):
            rows = slice(part * block, (part + 1) * block)
            shift = shifted_prior if is_prior(part) else scaled_peak
            weight = jnp.exp2(scores[rows] * factor - shift)
            total = total + jnp.sum(weight, axis=0, keepdims=True)
            scores[rows] = weight
        inverse = 1.0 / total
        attended = jnp.zeros((HDIM, block), F32)
        for part in range(parts):
            rows = slice(part * block, (part + 1) * block)
            weight = scores[rows].astype(BF16)
            attended = attended + matmul(values_t[:, rows_of(part)], weight)
        attended = (attended * inverse).astype(BF16)
        out_ref[0, here] = attended.T
        row_dot = jnp.sum(
            attended.astype(F32) * grad_t.astype(F32), axis=0, keepdims=True
        )
        query_grad = jnp.zeros((HDIM, block), F32)
        for part in range(parts):
            rows = slice(part * block, (part + 1) * block)
            probability = scores[rows] * inverse
            dprob = matmul(values[rows_of(part)], grad_t)
            dscore = (probability * (dprob - row_dot)).astype(BF16)
            query_grad = query_grad + matmul(keys_t[:, rows_of(part)], dscore)
            dkeys[rows_of(part)] += matmul(dscore, query)
            dvalues[rows_of(part)] += matmul(probability.astype(BF16), grad)
        dq_ref[0, here] = (query_grad * SCALING).astype(BF16).T
    dk_ref[0] = (dkeys[length:] * SCALING).astype(BF16)
    dv_ref[0] = dvalues[length:].astype(BF16)
    dprior_ref[0] = (dkeys[:length] * SCALING).astype(BF16)
    dprior_ref[1] = dvalues[:length].astype(BF16)


def row_heads(bias, arrays, prior):
    _, length, width = arrays[0].shape
    block = 256
    window = length + block
    one = pl.BlockSpec((1, length, HDIM), lambda h: (0, 0, h))
    two = pl.BlockSpec((2, length, HDIM), lambda h: (0, 0, h))
    shape = jax.ShapeDtypeStruct((1, length, width), BF16)
    return pl.pallas_call(
        functools.partial(row_kernel, block),
        grid=(HALF,),
        in_specs=[pl.BlockSpec(memory_space=pltpu.SMEM)] + [one] * 4 + [two],
        out_specs=[one] * 4 + [two],
        out_shape=[shape] * 4 + [jax.ShapeDtypeStruct(prior.shape, BF16)],
        scratch_shapes=[
            pltpu.VMEM((2 * length, HDIM), BF16),
            pltpu.VMEM((2 * length, HDIM), BF16),
            pltpu.VMEM((HDIM, 2 * length), BF16),
            pltpu.VMEM((HDIM, 2 * length), BF16),
            pltpu.VMEM((window, block), F32),
            pltpu.VMEM((2 * length, HDIM), F32),
            pltpu.VMEM((2 * length, HDIM), F32),
        ],
        compiler_params=params(40),
        cost_estimate=pl.CostEstimate(
            flops=12 * HALF * length * window * HDIM,
            bytes_accessed=24 * length * width // 2,
            transcendentals=HALF * length * window,
        ),
        name="row_heads",
    )(bias, *arrays, prior)


def column_kernel(in_ref, out_ref, query_all, key_all, value_all, grad_all):
    rows, _, per, _ = in_ref.shape
    staged = (query_all, key_all, value_all, grad_all)
    for at, ref in enumerate(staged):
        ref[...] = in_ref[:, at].astype(F32).reshape(rows * per, HDIM)
    key_at = lax.broadcasted_iota(jnp.int32, (rows, rows), 0)
    query_at = lax.broadcasted_iota(jnp.int32, (rows, rows), 1)
    causal = key_at <= query_at
    factor = SCALING * LOG2E
    for column in range(per):
        pick = pl.ds(column, rows, stride=per)
        query, key, value, grad = [ref[pick, :].astype(BF16) for ref in staged]
        score = jnp.where(causal, matmul_nt(key, query), NEG)
        peak = jnp.max(score, axis=0, keepdims=True)
        weight = jnp.exp2((score - peak) * factor)
        inverse = 1.0 / jnp.sum(weight, axis=0, keepdims=True)
        probability = weight * inverse
        low = probability.astype(BF16)
        dprob = matmul_nt(value, grad)
        row_dot = jnp.sum(probability * dprob, axis=0, keepdims=True)
        dscore = (probability * (dprob - row_dot)).astype(BF16)
        query_all[pick, :] = matmul_tn(low, value)
        key_all[pick, :] = matmul_tn(dscore, key) * SCALING
        value_all[pick, :] = matmul(dscore, query) * SCALING
        grad_all[pick, :] = matmul(low, grad)
    for at, ref in enumerate(staged):
        out_ref[:, at] = ref[...].reshape(rows, per, HDIM).astype(BF16)


def column_heads(arrived):
    rows, _, per, half = arrived.shape
    spec = pl.BlockSpec((rows, 4, per, HDIM), lambda h: (0, 0, 0, h))
    return pl.pallas_call(
        column_kernel,
        grid=(HALF,),
        in_specs=[spec],
        out_specs=spec,
        out_shape=jax.ShapeDtypeStruct(arrived.shape, BF16),
        scratch_shapes=[pltpu.VMEM((rows * per, HDIM), F32)] * 4,
        compiler_params=params(40),
        cost_estimate=pl.CostEstimate(
            flops=12 * HALF * per * rows * rows * HDIM,
            bytes_accessed=16 * rows * per * half,
            transcendentals=HALF * per * rows * rows,
        ),
        name="column_heads",
    )(arrived)


def place_kernel(cols_ref, back_ref, dk_in, dv_in, out_any, dq_any, out_ref, dq_ref, dk_ref, dv_ref):
    del out_any, dq_any
    half = out_ref.shape[2]
    flat = out_ref.shape[1:]
    out_ref[0] = cols_ref[:, 0].reshape(flat)
    dq_ref[0] = cols_ref[:, 1].reshape(flat)
    for at, (own, ref) in enumerate(((dk_in, dk_ref), (dv_in, dv_ref))):
        summed = own[0].astype(F32) + back_ref[at].astype(F32)
        ref[0, :, :half] = summed.astype(BF16)
        ref[0, :, half:] = cols_ref[:, 2 + at].reshape(flat)


def place(columns, back, row_out, row_dq, row_dk, row_dv):
    devices, _, per, half = columns.shape
    _, length, width = row_out.shape
    step = 16
    left = pl.BlockSpec((1, step * per, half), lambda i: (0, i, 0))
    right = pl.BlockSpec((1, step * per, half), lambda i: (0, i, 1))
    whole = pl.BlockSpec((1, step * per, width), lambda i: (0, i, 0))
    anywhere = pl.BlockSpec(memory_space=pl.ANY)
    shape = jax.ShapeDtypeStruct((1, length, width), BF16)
    return pl.pallas_call(
        place_kernel,
        grid=(devices // step,),
        in_specs=[
            pl.BlockSpec((step, 4, per, half), lambda i: (i, 0, 0, 0)),
            pl.BlockSpec((2, step * per, half), lambda i: (0, i, 0)),
            left,
            left,
            anywhere,
            anywhere,
        ],
        out_specs=[right, right, whole, whole],
        out_shape=[shape] * 4,
        input_output_aliases={4: 0, 5: 1, 2: 2, 3: 3},
        compiler_params=params(32),
        cost_estimate=pl.CostEstimate(
            flops=0, bytes_accessed=28 * length * half, transcendentals=0
        ),
        name="place",
    )(columns, back, row_dk, row_dv, row_out, row_dq)


def on_device(queries, key_vectors, value_vectors, out_cotangent):
    devices = lax.axis_size(AXES)
    half = queries.shape[2] // 2
    arrays = (queries, key_vectors, value_vectors, out_cotangent)
    last_pair = jnp.stack([key_vectors[0, :, :half], value_vectors[0, :, :half]])
    forward = [(i, i + 1) for i in range(devices - 1)]
    backward = [(i + 1, i) for i in range(devices - 1)]
    prior = lax.ppermute(last_pair, AXES, forward)
    packed = pack_columns(arrays, devices)
    arrived = lax.all_to_all(packed, AXES, split_axis=0, concat_axis=0, tiled=True)
    at_start = lax.axis_index(AXES) == 0
    bias = jnp.where(at_start, NEG, 0.0).astype(F32).reshape(1)
    row_out, row_dq, row_dk, row_dv, dprior = row_heads(bias, arrays, prior)
    leaving = column_heads(arrived)
    back = lax.ppermute(dprior, AXES, backward)
    returned = lax.all_to_all(leaving, AXES, split_axis=0, concat_axis=0, tiled=True)
    return tuple(place(returned, back, row_out, row_dq, row_dk, row_dv))


def solution(mesh):
    spec = P(AXES, None, None)
    return jax.shard_map(
        on_device, mesh=mesh, in_specs=(spec,) * 4, out_specs=(spec,) * 4, check_vma=False
    )
```

```python
import functools
import math

import jax
import jax.numpy as jnp
from jax import lax
from jax.experimental import pallas as pl
from jax.experimental.pallas import tpu as pltpu
from jax.sharding import PartitionSpec as P

HEADS = 8
HDIM = 128
HALF = HEADS // 2
SCALING = HDIM ** (-0.5)
LOG2E = math.log2(math.e)
NEG = -1e30
AHEAD = 1000
PIECES = 4
CHUNKS = 4
AXES = ("grp", "seq")
F32 = jnp.float32
BF16 = jnp.bfloat16


def matmul(lhs, rhs):
    return jnp.dot(lhs, rhs, preferred_element_type=F32)


def matmul_nt(lhs, rhs):
    return lax.dot_general(lhs, rhs, (((1,), (1,)), ((), ())), preferred_element_type=F32)


def matmul_tn(lhs, rhs):
    return lax.dot_general(lhs, rhs, (((0,), (0,)), ((), ())), preferred_element_type=F32)


def params():
    return pltpu.CompilerParams(vmem_limit_bytes=60 * 1024 * 1024)


def stream(moves, in_sems, out_sems):
    arriving = []
    for incoming, _ in moves:
        started = []
        for source, target in incoming:
            started.append(pltpu.make_async_copy(source, target, in_sems.at[len(arriving), len(started)]))
            started[-1].start()
        arriving.append(started)
    leaving = []
    for at, (_, outgoing) in enumerate(moves):
        for copy in arriving[at]:
            copy.wait()
        for source, target in outgoing:
            copy = pltpu.make_async_copy(source, target, out_sems.at[at, len(leaving) % len(outgoing)])
            copy.start()
            leaving.append(copy)
    for copy in leaving:
        copy.wait()


def pair_kernel(first, k_ref, v_ref, *refs):
    outs, (buffer, in_sems, out_sems) = refs[:-3], refs[-3:]
    wide = outs[0].shape[2]
    moves = []
    for piece, out in enumerate(outs):
        here = pl.ds(first * HDIM + piece * wide, wide)
        incoming = [
            (ref.at[0, :, here], buffer.at[piece, at]) for at, ref in enumerate((k_ref, v_ref))
        ]
        moves.append((incoming, [(buffer.at[piece], out)]))
    stream(moves, in_sems, out_sems)


def pack_pairs(key_vectors, value_vectors, first, pieces):
    _, length, width = key_vectors.shape
    wide = width // 2 // PIECES
    anywhere = pl.BlockSpec(memory_space=pl.ANY)
    return pl.pallas_call(
        functools.partial(pair_kernel, first),
        in_specs=[anywhere] * 2,
        out_specs=[anywhere] * pieces,
        out_shape=[jax.ShapeDtypeStruct((2, length, wide), BF16)] * pieces,
        scratch_shapes=[
            pltpu.VMEM((pieces, 2, length, wide), BF16),
            pltpu.SemaphoreType.DMA((pieces, 2)),
            pltpu.SemaphoreType.DMA((pieces, 1)),
        ],
        compiler_params=params(),
        cost_estimate=pl.CostEstimate(
            flops=0, bytes_accessed=8 * pieces * length * wide, transcendentals=0
        ),
        name="pack_pairs",
    )(key_vectors, value_vectors)


def pack_kernel(q_ref, k_ref, v_ref, g_ref, out_ref, buffer, in_sems, out_sems):
    devices, _, per, half = out_ref.shape
    count = devices // CHUNKS
    moves = []
    for chunk in range(CHUNKS):
        part = pl.ds(chunk * count, count)
        incoming = [
            (ref.at[part, :, pl.ds(half, half)], buffer.at[part, at])
            for at, ref in enumerate((q_ref, k_ref, v_ref, g_ref))
        ]
        moves.append((incoming, [(buffer.at[part], out_ref.at[part])]))
    stream(moves, in_sems, out_sems)


def pack_columns(arrays, devices):
    _, length, width = arrays[0].shape
    half = width // 2
    per = length // devices
    anywhere = pl.BlockSpec(memory_space=pl.ANY)
    shape = (devices, 4, per, half)
    return pl.pallas_call(
        pack_kernel,
        in_specs=[anywhere] * 4,
        out_specs=anywhere,
        out_shape=jax.ShapeDtypeStruct(shape, BF16),
        scratch_shapes=[
            pltpu.VMEM(shape, BF16),
            pltpu.SemaphoreType.DMA((CHUNKS, 4)),
            pltpu.SemaphoreType.DMA((CHUNKS, 1)),
        ],
        compiler_params=params(),
        cost_estimate=pl.CostEstimate(
            flops=0, bytes_accessed=16 * length * half, transcendentals=0
        ),
        name="pack_columns",
    )(*[array.reshape(devices, per, width) for array in arrays])


def row_kernel(block, made, bias_ref, q_ref, k_ref, v_ref, g_ref, prior_ref, *refs):
    out_ref, dq_ref, dk_ref, dv_ref, dk_prior, dv_prior = refs[made : made + 6]
    keys, values, keys_t, values_t, scores, dkeys, dvalues = refs[made + 6 :]
    length = q_ref.shape[1]
    window = length + block
    parts = window // block
    keys[:length] = prior_ref[0]
    keys[length:] = k_ref[0]
    values[:length] = prior_ref[1]
    values[length:] = v_ref[0]
    for at in range(0, 2 * length, block):
        rows = slice(at, at + block)
        keys_t[:, rows] = keys[rows].T
        values_t[:, rows] = values[rows].T
    dkeys[...] = jnp.zeros_like(dkeys)
    dvalues[...] = jnp.zeros_like(dvalues)
    bias = bias_ref[0]
    key_at = lax.broadcasted_iota(jnp.int32, (block, block), 0)
    query_at = lax.broadcasted_iota(jnp.int32, (block, block), 1)
    older = key_at > query_at
    for qi in range(length // block):
        here = slice(qi * block, (qi + 1) * block)
        query = q_ref[0, here]
        grad = g_ref[0, here]
        query_t = query.T
        grad_t = grad.T

        def rows_of(part):
            start = qi * block + part * block
            return slice(start, start + block)

        def is_prior(part):
            return (qi + part) * block < length

        peak = jnp.full((1, block), NEG, F32)
        for part in range(parts):
            score = matmul(keys[rows_of(part)], query_t)
            if part == 0:
                score = jnp.where(older, score, NEG)
            if part == parts - 1:
                score = jnp.where(older, NEG, score)
            top = jnp.max(score, axis=0, keepdims=True)
            if is_prior(part):
                top = top + bias
            peak = jnp.maximum(peak, top)
            scores[part * block : (part + 1) * block] = score
        factor = SCALING * LOG2E
        scaled_peak = peak * factor
        shifted_prior = (peak - bias) * factor
        total = jnp.zeros((1, block), F32)
        for part in range(parts):
            rows = slice(part * block, (part + 1) * block)
            shift = shifted_prior if is_prior(part) else scaled_peak
            weight = jnp.exp2(scores[rows] * factor - shift)
            total = total + jnp.sum(weight, axis=0, keepdims=True)
            scores[rows] = weight
        inverse = 1.0 / total
        attended = jnp.zeros((HDIM, block), F32)
        for part in range(parts):
            rows = slice(part * block, (part + 1) * block)
            weight = scores[rows].astype(BF16)
            attended = attended + matmul(values_t[:, rows_of(part)], weight)
        attended = (attended * inverse).astype(BF16)
        out_ref[0, here] = attended.T
        row_dot = jnp.sum(
            attended.astype(F32) * grad_t.astype(F32), axis=0, keepdims=True
        )
        query_grad = jnp.zeros((HDIM, block), F32)
        for part in range(parts):
            rows = slice(part * block, (part + 1) * block)
            probability = scores[rows] * inverse
            dprob = matmul(values[rows_of(part)], grad_t)
            dscore = (probability * (dprob - row_dot)).astype(BF16)
            query_grad = query_grad + matmul(keys_t[:, rows_of(part)], dscore)
            dkeys[rows_of(part)] += matmul(dscore, query)
            dvalues[rows_of(part)] += matmul(probability.astype(BF16), grad)
        dq_ref[0, here] = (query_grad * SCALING).astype(BF16).T
    dk_ref[0] = (dkeys[length:] * SCALING).astype(BF16)
    dv_ref[0] = dvalues[length:].astype(BF16)
    dk_prior[0] = (dkeys[:length] * SCALING).astype(BF16)
    dv_prior[0] = dvalues[:length].astype(BF16)


def row_heads(piece, bias, arrays, prior, made):
    _, length, width = arrays[0].shape
    block = 256
    window = length + block
    heads = HALF // PIECES
    one = pl.BlockSpec((1, length, HDIM), lambda h: (0, 0, piece * heads + h))
    two = pl.BlockSpec((2, length, HDIM), lambda h: (0, 0, h))
    shape = jax.ShapeDtypeStruct((1, length, width), BF16)
    partial_shape = jax.ShapeDtypeStruct((1, length, HALF * HDIM), BF16)
    return pl.pallas_call(
        functools.partial(row_kernel, block, len(made)),
        grid=(heads,),
        in_specs=[pl.BlockSpec(memory_space=pltpu.SMEM)]
        + [one] * 4
        + [two]
        + [pl.BlockSpec(memory_space=pl.ANY)] * len(made),
        out_specs=[one] * 6,
        out_shape=[shape] * 4 + [partial_shape] * 2,
        input_output_aliases={6 + at: at for at in range(len(made))},
        scratch_shapes=[
            pltpu.VMEM((2 * length, HDIM), BF16),
            pltpu.VMEM((2 * length, HDIM), BF16),
            pltpu.VMEM((HDIM, 2 * length), BF16),
            pltpu.VMEM((HDIM, 2 * length), BF16),
            pltpu.VMEM((window, block), F32),
            pltpu.VMEM((2 * length, HDIM), F32),
            pltpu.VMEM((2 * length, HDIM), F32),
        ],
        compiler_params=params(),
        cost_estimate=pl.CostEstimate(
            flops=AHEAD * heads * length * window * HDIM,
            bytes_accessed=24 * heads * length * HDIM,
            transcendentals=heads * length * window,
        ),
        name="row_heads",
    )(bias, *arrays, prior, *made)


def column_kernel(in_ref, out_ref, *scratch):
    rows, _, per, _ = in_ref.shape
    staged, results = scratch[:4], scratch[4:]
    for at, ref in enumerate(staged):
        ref[...] = in_ref[:, at].astype(F32).reshape(rows * per, HDIM)
    key_at = lax.broadcasted_iota(jnp.int32, (rows, rows), 0)
    query_at = lax.broadcasted_iota(jnp.int32, (rows, rows), 1)
    causal = key_at <= query_at
    factor = SCALING * LOG2E
    columns = range(per)
    picks = [pl.ds(column, rows, stride=per) for column in columns]
    query, key, value, grad = [
        [ref[pick, :].astype(BF16) for pick in picks] for ref in staged
    ]
    score = [jnp.where(causal, matmul_nt(key[c], query[c]), NEG) for c in columns]
    dprob = [matmul_nt(value[c], grad[c]) for c in columns]
    peak = [jnp.max(score[c], axis=0, keepdims=True) for c in columns]
    weight = [jnp.exp2((score[c] - peak[c]) * factor) for c in columns]
    inverse = [1.0 / jnp.sum(weight[c], axis=0, keepdims=True) for c in columns]
    probability = [weight[c] * inverse[c] for c in columns]
    low = [probability[c].astype(BF16) for c in columns]
    row_dot = [jnp.sum(probability[c] * dprob[c], axis=0, keepdims=True) for c in columns]
    dscore = [(probability[c] * (dprob[c] - row_dot[c])).astype(BF16) for c in columns]
    for c in columns:
        results[0][picks[c], :] = matmul_tn(low[c], value[c])
    for c in columns:
        results[3][picks[c], :] = matmul(low[c], grad[c])
    for c in columns:
        results[1][picks[c], :] = matmul_tn(dscore[c], key[c]) * SCALING
    for c in columns:
        results[2][picks[c], :] = matmul(dscore[c], query[c]) * SCALING
    for at, ref in enumerate(results):
        out_ref[:, at] = ref[...].reshape(rows, per, HDIM).astype(BF16)


def column_heads(arrived):
    rows, _, per, half = arrived.shape
    spec = pl.BlockSpec((rows, 4, per, HDIM), lambda h: (0, 0, 0, h))
    return pl.pallas_call(
        column_kernel,
        grid=(HALF,),
        in_specs=[spec],
        out_specs=spec,
        out_shape=jax.ShapeDtypeStruct(arrived.shape, BF16),
        scratch_shapes=[pltpu.VMEM((rows * per, HDIM), F32)] * 8,
        compiler_params=params(),
        cost_estimate=pl.CostEstimate(
            flops=12 * HALF * per * rows * rows * HDIM,
            bytes_accessed=16 * rows * per * half,
            transcendentals=HALF * per * rows * rows,
        ),
        name="column_heads",
    )(arrived)


def add_kernel(dk_back, dv_back, dk_in, dv_in, dk_ref, dv_ref):
    dk_ref[0] = (dk_in[0].astype(F32) + dk_back[0].astype(F32)).astype(BF16)
    dv_ref[0] = (dv_in[0].astype(F32) + dv_back[0].astype(F32)).astype(BF16)


def add_returned(back, row_dk, row_dv):
    _, length, half = back[0].shape
    rows = 512
    left = pl.BlockSpec((1, rows, half), lambda i: (0, i, 0))
    shape = jax.ShapeDtypeStruct(row_dk.shape, BF16)
    return pl.pallas_call(
        add_kernel,
        grid=(length // rows,),
        in_specs=[left] * 4,
        out_specs=[left, left],
        out_shape=[shape] * 2,
        input_output_aliases={2: 0, 3: 1},
        compiler_params=params(),
        cost_estimate=pl.CostEstimate(
            flops=100 * AHEAD * length * HDIM * HDIM,
            bytes_accessed=12 * length * half,
            transcendentals=0,
        ),
        name="add_returned",
    )(*back, row_dk, row_dv)


def place_kernel(cols_ref, *refs):
    outs, (buffer, in_sems, out_sems) = refs[4:8], refs[8:]
    devices, _, per, half = cols_ref.shape
    count = devices // CHUNKS
    moves = []
    for chunk in range(CHUNKS):
        part = pl.ds(chunk * count, count)
        outgoing = [
            (buffer.at[part, at], out.at[part, :, pl.ds(half, half)])
            for at, out in enumerate(outs)
        ]
        moves.append(([(cols_ref.at[part], buffer.at[part])], outgoing))
    stream(moves, in_sems, out_sems)


def place(columns, rowwise):
    devices, _, per, half = columns.shape
    whole = rowwise[0].shape
    shape = (devices, per, whole[2])
    anywhere = pl.BlockSpec(memory_space=pl.ANY)
    placed = pl.pallas_call(
        place_kernel,
        in_specs=[anywhere] * 5,
        out_specs=[anywhere] * 4,
        out_shape=[jax.ShapeDtypeStruct(shape, BF16)] * 4,
        input_output_aliases={1: 0, 2: 1, 3: 2, 4: 3},
        scratch_shapes=[
            pltpu.VMEM(columns.shape, BF16),
            pltpu.SemaphoreType.DMA((CHUNKS, 1)),
            pltpu.SemaphoreType.DMA((CHUNKS, 4)),
        ],
        compiler_params=params(),
        cost_estimate=pl.CostEstimate(
            flops=0, bytes_accessed=16 * devices * per * half, transcendentals=0
        ),
        name="place",
    )(columns, *[array.reshape(shape) for array in rowwise])
    return [array.reshape(whole) for array in placed]


def on_device(queries, key_vectors, value_vectors, out_cotangent):
    devices = lax.axis_size(AXES)
    arrays = (queries, key_vectors, value_vectors, out_cotangent)
    forward = [(i, i + 1) for i in range(devices - 1)]
    backward = [(i + 1, i) for i in range(devices - 1)]
    last = PIECES - 1
    pairs = pack_pairs(key_vectors, value_vectors, 0, last)
    prior = [lax.ppermute(pair, AXES, forward) for pair in pairs]
    keys, values, _ = lax.optimization_barrier((key_vectors, value_vectors, prior[0]))
    pair = pack_pairs(keys, values, last * (HALF // PIECES), 1)[0]
    prior.append(lax.ppermute(pair, AXES, forward))
    packed = pack_columns(arrays, devices)
    packed, *_ = lax.optimization_barrier((packed, *prior[:2]))
    arrived = lax.all_to_all(packed, AXES, split_axis=0, concat_axis=0, tiled=True)
    at_start = lax.axis_index(AXES) == 0
    bias = jnp.where(at_start, NEG, 0.0).astype(F32).reshape(1)
    made = ()
    for piece in range(PIECES):
        made = row_heads(piece, bias, arrays, prior[piece], made)
    row_out, row_dq, row_dk, row_dv, *partials = made
    arrived, *partials = lax.optimization_barrier((arrived, *partials))
    back = [lax.ppermute(partial, AXES, backward) for partial in partials]
    leaving = column_heads(arrived)
    leaving, _ = lax.optimization_barrier((leaving, back[0]))
    returned = lax.all_to_all(leaving, AXES, split_axis=0, concat_axis=0, tiled=True)
    row_dk, row_dv = add_returned(back, row_dk, row_dv)
    return tuple(place(returned, (row_out, row_dq, row_dk, row_dv)))


def solution(mesh):
    spec = P(AXES, None, None)
    return jax.shard_map(
        on_device, mesh=mesh, in_specs=(spec,) * 4, out_specs=(spec,) * 4, check_vma=False
    )
```

```python
import functools
import itertools
import math

import jax
import jax.numpy as jnp
from jax import lax
from jax.experimental import pallas as pl
from jax.experimental.pallas import tpu as pltpu
from jax.sharding import PartitionSpec as P

HEADS = 8
HDIM = 128
HALF = HEADS // 2
SCALING = HDIM ** (-0.5)
LOG2E = math.log2(math.e)
NEG = -1e30
AHEAD = 1000
PIECES = 4
CHUNKS = 4
VMEM_BYTES = 64 * 1024 * 1024 - 256 * 1024
AXES = ("grp", "seq")
F32 = jnp.float32
BF16 = jnp.bfloat16


def matmul(lhs, rhs):
    return jnp.dot(lhs, rhs, preferred_element_type=F32)


def matmul_nt(lhs, rhs):
    return lax.dot_general(lhs, rhs, (((1,), (1,)), ((), ())), preferred_element_type=F32)


def matmul_tn(lhs, rhs):
    return lax.dot_general(lhs, rhs, (((0,), (0,)), ((), ())), preferred_element_type=F32)


def params():
    return pltpu.CompilerParams(vmem_limit_bytes=VMEM_BYTES)


def stream(moves, in_sems, out_sems):
    arriving = []
    for incoming, _ in moves:
        started = []
        for source, target in incoming:
            started.append(pltpu.make_async_copy(source, target, in_sems.at[len(arriving), len(started)]))
            started[-1].start()
        arriving.append(started)
    leaving = []
    for at, (_, outgoing) in enumerate(moves):
        for copy in arriving[at]:
            copy.wait()
        for source, target in outgoing:
            copy = pltpu.make_async_copy(source, target, out_sems.at[at, len(leaving) % len(outgoing)])
            copy.start()
            leaving.append(copy)
    for copy in leaving:
        copy.wait()


def pair_kernel(first, k_ref, v_ref, *refs):
    outs, (buffer, in_sems, out_sems) = refs[:-3], refs[-3:]
    wide = outs[0].shape[2]
    moves = []
    for piece, out in enumerate(outs):
        here = pl.ds(first * HDIM + piece * wide, wide)
        incoming = [
            (ref.at[0, :, here], buffer.at[piece, at]) for at, ref in enumerate((k_ref, v_ref))
        ]
        moves.append((incoming, [(buffer.at[piece], out)]))
    stream(moves, in_sems, out_sems)


def pack_pairs(key_vectors, value_vectors, first, pieces):
    _, length, width = key_vectors.shape
    wide = width // 2 // PIECES
    anywhere = pl.BlockSpec(memory_space=pl.ANY)
    return pl.pallas_call(
        functools.partial(pair_kernel, first),
        in_specs=[anywhere] * 2,
        out_specs=[anywhere] * pieces,
        out_shape=[jax.ShapeDtypeStruct((2, length, wide), BF16)] * pieces,
        scratch_shapes=[
            pltpu.VMEM((pieces, 2, length, wide), BF16),
            pltpu.SemaphoreType.DMA((pieces, 2)),
            pltpu.SemaphoreType.DMA((pieces, 1)),
        ],
        compiler_params=params(),
        cost_estimate=pl.CostEstimate(
            flops=0, bytes_accessed=8 * pieces * length * wide, transcendentals=0
        ),
        name="pack_pairs",
    )(key_vectors, value_vectors)


def pack_kernel(q_ref, k_ref, v_ref, g_ref, out_ref, buffer, in_sems, out_sems):
    devices, _, per, half = out_ref.shape
    count = devices // CHUNKS
    moves = []
    for chunk in range(CHUNKS):
        part = pl.ds(chunk * count, count)
        incoming = [
            (ref.at[part, :, pl.ds(half, half)], buffer.at[part, at])
            for at, ref in enumerate((q_ref, k_ref, v_ref, g_ref))
        ]
        moves.append((incoming, [(buffer.at[part], out_ref.at[part])]))
    stream(moves, in_sems, out_sems)


def pack_columns(arrays, devices):
    _, length, width = arrays[0].shape
    half = width // 2
    per = length // devices
    anywhere = pl.BlockSpec(memory_space=pl.ANY)
    shape = (devices, 4, per, half)
    return pl.pallas_call(
        pack_kernel,
        in_specs=[anywhere] * 4,
        out_specs=anywhere,
        out_shape=jax.ShapeDtypeStruct(shape, BF16),
        scratch_shapes=[
            pltpu.VMEM(shape, BF16),
            pltpu.SemaphoreType.DMA((CHUNKS, 4)),
            pltpu.SemaphoreType.DMA((CHUNKS, 1)),
        ],
        compiler_params=params(),
        cost_estimate=pl.CostEstimate(
            flops=0, bytes_accessed=16 * length * half, transcendentals=0
        ),
        name="pack_columns",
    )(*[array.reshape(devices, per, width) for array in arrays])


def row_kernel(block, made, bias_ref, q_ref, k_ref, v_ref, g_ref, prior_ref, *refs):
    out_ref, dq_ref, dk_ref, dv_ref, dk_prior, dv_prior = refs[made : made + 6]
    keys, values, keys_t, values_t, scores, dkeys, dvalues = refs[made + 6 :]
    length = q_ref.shape[1]
    window = length + block
    parts = window // block
    keys[:length] = prior_ref[0]
    keys[length:] = k_ref[0]
    values[:length] = prior_ref[1]
    values[length:] = v_ref[0]
    for at in range(0, 2 * length, block):
        rows = slice(at, at + block)
        keys_t[:, rows] = keys[rows].T
        values_t[:, rows] = values[rows].T
    dkeys[...] = jnp.zeros_like(dkeys)
    dvalues[...] = jnp.zeros_like(dvalues)
    bias = bias_ref[0]
    key_at = lax.broadcasted_iota(jnp.int32, (block, block), 0)
    query_at = lax.broadcasted_iota(jnp.int32, (block, block), 1)
    older = key_at > query_at
    for qi in range(length // block):
        here = slice(qi * block, (qi + 1) * block)
        query = q_ref[0, here]
        grad = g_ref[0, here]
        query_t = query.T
        grad_t = grad.T

        def rows_of(part):
            start = qi * block + part * block
            return slice(start, start + block)

        def is_prior(part):
            return (qi + part) * block < length

        peak = jnp.full((1, block), NEG, F32)
        for part in range(parts):
            score = matmul(keys[rows_of(part)], query_t)
            if part == 0:
                score = jnp.where(older, score, NEG)
            if part == parts - 1:
                score = jnp.where(older, NEG, score)
            top = jnp.max(score, axis=0, keepdims=True)
            if is_prior(part):
                top = top + bias
            peak = jnp.maximum(peak, top)
            scores[part * block : (part + 1) * block] = score
        factor = SCALING * LOG2E
        scaled_peak = peak * factor
        shifted_prior = (peak - bias) * factor
        total = jnp.zeros((1, block), F32)
        for part in range(parts):
            rows = slice(part * block, (part + 1) * block)
            shift = shifted_prior if is_prior(part) else scaled_peak
            weight = jnp.exp2(scores[rows] * factor - shift)
            total = total + jnp.sum(weight, axis=0, keepdims=True)
            scores[rows] = weight
        inverse = 1.0 / total
        attended = jnp.zeros((HDIM, block), F32)
        for part in range(parts):
            rows = slice(part * block, (part + 1) * block)
            weight = scores[rows].astype(BF16)
            attended = attended + matmul(values_t[:, rows_of(part)], weight)
        attended = (attended * inverse).astype(BF16)
        out_ref[0, here] = attended.T
        row_dot = jnp.sum(
            attended.astype(F32) * grad_t.astype(F32), axis=0, keepdims=True
        )
        query_grad = jnp.zeros((HDIM, block), F32)
        for part in range(parts):
            rows = slice(part * block, (part + 1) * block)
            probability = scores[rows] * inverse
            dprob = matmul(values[rows_of(part)], grad_t)
            dscore = (probability * (dprob - row_dot)).astype(BF16)
            query_grad = query_grad + matmul(keys_t[:, rows_of(part)], dscore)
            dkeys[rows_of(part)] += matmul(dscore, query)
            dvalues[rows_of(part)] += matmul(probability.astype(BF16), grad)
        dq_ref[0, here] = (query_grad * SCALING).astype(BF16).T
    dk_ref[0] = (dkeys[length:] * SCALING).astype(BF16)
    dv_ref[0] = dvalues[length:].astype(BF16)
    dk_prior[0] = (dkeys[:length] * SCALING).astype(BF16)
    dv_prior[0] = dvalues[:length].astype(BF16)


def row_heads(piece, bias, arrays, prior, made):
    _, length, width = arrays[0].shape
    block = 256
    window = length + block
    heads = HALF // PIECES
    one = pl.BlockSpec((1, length, HDIM), lambda h: (0, 0, piece * heads + h))
    two = pl.BlockSpec((2, length, HDIM), lambda h: (0, 0, h))
    shape = jax.ShapeDtypeStruct((1, length, width), BF16)
    partial_shape = jax.ShapeDtypeStruct((1, length, HALF * HDIM), BF16)
    return pl.pallas_call(
        functools.partial(row_kernel, block, len(made)),
        grid=(heads,),
        in_specs=[pl.BlockSpec(memory_space=pltpu.SMEM)]
        + [one] * 4
        + [two]
        + [pl.BlockSpec(memory_space=pl.ANY)] * len(made),
        out_specs=[one] * 6,
        out_shape=[shape] * 4 + [partial_shape] * 2,
        input_output_aliases={6 + at: at for at in range(len(made))},
        scratch_shapes=[
            pltpu.VMEM((2 * length, HDIM), BF16),
            pltpu.VMEM((2 * length, HDIM), BF16),
            pltpu.VMEM((HDIM, 2 * length), BF16),
            pltpu.VMEM((HDIM, 2 * length), BF16),
            pltpu.VMEM((window, block), F32),
            pltpu.VMEM((2 * length, HDIM), F32),
            pltpu.VMEM((2 * length, HDIM), F32),
        ],
        compiler_params=params(),
        cost_estimate=pl.CostEstimate(
            flops=AHEAD * heads * length * window * HDIM,
            bytes_accessed=24 * heads * length * HDIM,
            transcendentals=heads * length * window,
        ),
        name="row_heads",
    )(bias, *arrays, prior, *made)


def column_kernel(row_down, row_across, in_ref, out_ref, *scratch):
    rows, _, per, _ = in_ref.shape
    staged, results = scratch[:4], scratch[4:]
    for at, ref in enumerate(staged):
        ref[...] = in_ref[:, at].astype(F32).reshape(rows * per, HDIM)
    causal = row_down[...] <= row_across[...]
    factor = SCALING * LOG2E
    columns = range(per)
    picks = [pl.ds(column, rows, stride=per) for column in columns]
    query, key, value, grad = [
        [ref[pick, :].astype(BF16) for pick in picks] for ref in staged
    ]
    score = [jnp.where(causal, matmul_nt(key[c], query[c]), NEG) for c in columns]
    dprob = [matmul_nt(value[c], grad[c]) for c in columns]
    peak = [jnp.max(score[c], axis=0, keepdims=True) for c in columns]
    weight = [jnp.exp2((score[c] - peak[c]) * factor) for c in columns]
    inverse = [1.0 / jnp.sum(weight[c], axis=0, keepdims=True) for c in columns]
    probability = [weight[c] * inverse[c] for c in columns]
    low = [probability[c].astype(BF16) for c in columns]
    row_dot = [jnp.sum(probability[c] * dprob[c], axis=0, keepdims=True) for c in columns]
    dscore = [(probability[c] * (dprob[c] - row_dot[c])).astype(BF16) for c in columns]
    for c in columns:
        results[0][picks[c], :] = matmul_tn(low[c], value[c])
    for c in columns:
        results[3][picks[c], :] = matmul(low[c], grad[c])
    for c in columns:
        results[1][picks[c], :] = matmul_tn(dscore[c], key[c]) * SCALING
    for c in columns:
        results[2][picks[c], :] = matmul(dscore[c], query[c]) * SCALING
    for at, ref in enumerate(results):
        out_ref[:, at] = ref[...].reshape(rows, per, HDIM).astype(BF16)


def column_heads(arrived, order):
    rows, _, per, half = arrived.shape
    row_ids = jnp.array(order, jnp.int32)
    spec = pl.BlockSpec((rows, 4, per, HDIM), lambda h: (0, 0, 0, h))
    return pl.pallas_call(
        column_kernel,
        grid=(HALF,),
        in_specs=[
            pl.BlockSpec((rows, 1), lambda h: (0, 0)),
            pl.BlockSpec((1, rows), lambda h: (0, 0)),
            spec,
        ],
        out_specs=spec,
        out_shape=jax.ShapeDtypeStruct(arrived.shape, BF16),
        scratch_shapes=[pltpu.VMEM((rows * per, HDIM), F32)] * 8,
        compiler_params=params(),
        cost_estimate=pl.CostEstimate(
            flops=12 * HALF * per * rows * rows * HDIM,
            bytes_accessed=16 * rows * per * half,
            transcendentals=HALF * per * rows * rows,
        ),
        name="column_heads",
    )(row_ids[:, None], row_ids[None, :], arrived)


def add_kernel(dk_back, dv_back, dk_in, dv_in, dk_ref, dv_ref):
    dk_ref[0] = (dk_in[0].astype(F32) + dk_back[0].astype(F32)).astype(BF16)
    dv_ref[0] = (dv_in[0].astype(F32) + dv_back[0].astype(F32)).astype(BF16)


def add_returned(back, row_dk, row_dv):
    _, length, half = back[0].shape
    rows = 512
    left = pl.BlockSpec((1, rows, half), lambda i: (0, i, 0))
    shape = jax.ShapeDtypeStruct(row_dk.shape, BF16)
    return pl.pallas_call(
        add_kernel,
        grid=(length // rows,),
        in_specs=[left] * 4,
        out_specs=[left, left],
        out_shape=[shape] * 2,
        input_output_aliases={2: 0, 3: 1},
        compiler_params=params(),
        cost_estimate=pl.CostEstimate(
            flops=100 * AHEAD * length * HDIM * HDIM,
            bytes_accessed=12 * length * half,
            transcendentals=0,
        ),
        name="add_returned",
    )(*back, row_dk, row_dv)


def place_kernel(cols_ref, *refs):
    outs, (buffer, in_sems, out_sems) = refs[4:8], refs[8:]
    devices, _, per, half = cols_ref.shape
    count = devices // CHUNKS
    moves = []
    for chunk in range(CHUNKS):
        part = pl.ds(chunk * count, count)
        outgoing = [
            (buffer.at[part, at], out.at[part, :, pl.ds(half, half)])
            for at, out in enumerate(outs)
        ]
        moves.append(([(cols_ref.at[part], buffer.at[part])], outgoing))
    stream(moves, in_sems, out_sems)


def place(columns, rowwise):
    devices, _, per, half = columns.shape
    whole = rowwise[0].shape
    shape = (devices, per, whole[2])
    anywhere = pl.BlockSpec(memory_space=pl.ANY)
    placed = pl.pallas_call(
        place_kernel,
        in_specs=[anywhere] * 5,
        out_specs=[anywhere] * 4,
        out_shape=[jax.ShapeDtypeStruct(shape, BF16)] * 4,
        input_output_aliases={1: 0, 2: 1, 3: 2, 4: 3},
        scratch_shapes=[
            pltpu.VMEM(columns.shape, BF16),
            pltpu.SemaphoreType.DMA((CHUNKS, 1)),
            pltpu.SemaphoreType.DMA((CHUNKS, 4)),
        ],
        compiler_params=params(),
        cost_estimate=pl.CostEstimate(
            flops=0, bytes_accessed=16 * devices * per * half, transcendentals=0
        ),
        name="place",
    )(columns, *[array.reshape(shape) for array in rowwise])
    return [array.reshape(whole) for array in placed]


def exchange_order():
    order = []
    for z_hi, z_lo, y, x, core in itertools.product(range(2), range(2), range(4), range(4), range(2)):
        order.append(((z_hi * 4 + y) * 4 + x) * 4 + z_lo * 2 + core)
    return order


def exchange(blocks, order):
    return lax.all_to_all(
        blocks, AXES, split_axis=0, concat_axis=0, axis_index_groups=[order], tiled=True
    )


def on_device(queries, key_vectors, value_vectors, out_cotangent):
    devices = lax.axis_size(AXES)
    order = exchange_order()
    arrays = (queries, key_vectors, value_vectors, out_cotangent)
    forward = [(i, i + 1) for i in range(devices - 1)]
    backward = [(i + 1, i) for i in range(devices - 1)]
    last = PIECES - 1
    pairs = pack_pairs(key_vectors, value_vectors, 0, last)
    prior = [lax.ppermute(pair, AXES, forward) for pair in pairs]
    keys, values, _ = lax.optimization_barrier((key_vectors, value_vectors, prior[0]))
    pair = pack_pairs(keys, values, last * (HALF // PIECES), 1)[0]
    prior.append(lax.ppermute(pair, AXES, forward))
    packed = pack_columns(arrays, devices)
    packed, _ = lax.optimization_barrier((packed, prior[0]))
    arrived = exchange(packed, order)
    at_start = lax.axis_index(AXES) == 0
    bias = jnp.where(at_start, NEG, 0.0).astype(F32).reshape(1)
    made = ()
    for piece in range(PIECES):
        made = row_heads(piece, bias, arrays, prior[piece], made)
    row_out, row_dq, row_dk, row_dv, *partials = made
    arrived, *partials = lax.optimization_barrier((arrived, *partials))
    back = [lax.ppermute(partial, AXES, backward) for partial in partials]
    leaving = column_heads(arrived, order)
    leaving, _ = lax.optimization_barrier((leaving, back[0]))
    returned = exchange(leaving, order)
    row_dk, row_dv = add_returned(back, row_dk, row_dv)
    return tuple(place(returned, (row_out, row_dq, row_dk, row_dv)))


def solution(mesh):
    spec = P(AXES, None, None)
    return jax.shard_map(
        on_device, mesh=mesh, in_specs=(spec,) * 4, out_specs=(spec,) * 4, check_vma=False
    )
```

```python
import functools
import itertools
import math

import jax
import jax.numpy as jnp
from jax import lax
from jax.experimental import pallas as pl
from jax.experimental.pallas import tpu as pltpu
from jax.sharding import PartitionSpec as P

HEADS = 8
HDIM = 128
HALF = HEADS // 2
SCALING = HDIM ** (-0.5)
LOG2E = math.log2(math.e)
NEG = -1e30
AHEAD = 1000
PIECES = 2
CHUNKS = 4
VMEM_BYTES = 64 * 1024 * 1024 - 256 * 1024
AXES = ("grp", "seq")
F32 = jnp.float32
BF16 = jnp.bfloat16


def matmul(lhs, rhs):
    return jnp.dot(lhs, rhs, preferred_element_type=F32)


def matmul_nt(lhs, rhs):
    return lax.dot_general(lhs, rhs, (((1,), (1,)), ((), ())), preferred_element_type=F32)


def matmul_tn(lhs, rhs):
    return lax.dot_general(lhs, rhs, (((0,), (0,)), ((), ())), preferred_element_type=F32)


def params():
    return pltpu.CompilerParams(vmem_limit_bytes=VMEM_BYTES)


def stream(moves, in_sems, out_sems):
    arriving = []
    for incoming, _ in moves:
        started = []
        for source, target in incoming:
            started.append(pltpu.make_async_copy(source, target, in_sems.at[len(arriving), len(started)]))
            started[-1].start()
        arriving.append(started)
    leaving = []
    for at, (_, outgoing) in enumerate(moves):
        for copy in arriving[at]:
            copy.wait()
        for source, target in outgoing:
            copy = pltpu.make_async_copy(source, target, out_sems.at[at, len(leaving) % len(outgoing)])
            copy.start()
            leaving.append(copy)
    for copy in leaving:
        copy.wait()


def pair_kernel(k_ref, v_ref, *refs):
    outs, (buffer, in_sems, out_sems) = refs[:-3], refs[-3:]
    wide = outs[0].shape[2]
    moves = []
    for piece, out in enumerate(outs):
        here = pl.ds(piece * wide, wide)
        incoming = [
            (ref.at[0, :, here], buffer.at[piece, at]) for at, ref in enumerate((k_ref, v_ref))
        ]
        moves.append((incoming, [(buffer.at[piece], out)]))
    stream(moves, in_sems, out_sems)


def pack_pairs(key_vectors, value_vectors):
    _, length, width = key_vectors.shape
    wide = width // 2 // PIECES
    anywhere = pl.BlockSpec(memory_space=pl.ANY)
    return pl.pallas_call(
        pair_kernel,
        in_specs=[anywhere] * 2,
        out_specs=[anywhere] * PIECES,
        out_shape=[jax.ShapeDtypeStruct((2, length, wide), BF16)] * PIECES,
        scratch_shapes=[
            pltpu.VMEM((PIECES, 2, length, wide), BF16),
            pltpu.SemaphoreType.DMA((PIECES, 2)),
            pltpu.SemaphoreType.DMA((PIECES, 1)),
        ],
        compiler_params=params(),
        cost_estimate=pl.CostEstimate(
            flops=0, bytes_accessed=8 * PIECES * length * wide, transcendentals=0
        ),
        name="pack_pairs",
    )(key_vectors, value_vectors)


def pack_kernel(q_ref, k_ref, v_ref, g_ref, out_ref, buffer, in_sems, out_sems):
    devices, _, per, half = out_ref.shape
    count = devices // CHUNKS
    moves = []
    for chunk in range(CHUNKS):
        part = pl.ds(chunk * count, count)
        incoming = [
            (ref.at[part, :, pl.ds(half, half)], buffer.at[part, at])
            for at, ref in enumerate((q_ref, k_ref, v_ref, g_ref))
        ]
        moves.append((incoming, [(buffer.at[part], out_ref.at[part])]))
    stream(moves, in_sems, out_sems)


def pack_columns(arrays, devices):
    _, length, width = arrays[0].shape
    half = width // 2
    per = length // devices
    anywhere = pl.BlockSpec(memory_space=pl.ANY)
    shape = (devices, 4, per, half)
    return pl.pallas_call(
        pack_kernel,
        in_specs=[anywhere] * 4,
        out_specs=anywhere,
        out_shape=jax.ShapeDtypeStruct(shape, BF16),
        scratch_shapes=[
            pltpu.VMEM(shape, BF16),
            pltpu.SemaphoreType.DMA((CHUNKS, 4)),
            pltpu.SemaphoreType.DMA((CHUNKS, 1)),
        ],
        compiler_params=params(),
        cost_estimate=pl.CostEstimate(
            flops=0, bytes_accessed=16 * length * half, transcendentals=0
        ),
        name="pack_columns",
    )(*[array.reshape(devices, per, width) for array in arrays])


def row_kernel(block, made, bias_ref, q_ref, k_ref, v_ref, g_ref, prior_ref, *refs):
    out_ref, dq_ref, dk_ref, dv_ref, dk_prior, dv_prior = refs[made : made + 6]
    keys, values, keys_t, values_t, scores, dkeys, dvalues = refs[made + 6 :]
    length = q_ref.shape[1]
    window = length + block
    parts = window // block
    keys[:length] = prior_ref[0]
    keys[length:] = k_ref[0]
    values[:length] = prior_ref[1]
    values[length:] = v_ref[0]
    for at in range(0, 2 * length, block):
        rows = slice(at, at + block)
        keys_t[:, rows] = keys[rows].T
        values_t[:, rows] = values[rows].T
    dkeys[...] = jnp.zeros_like(dkeys)
    dvalues[...] = jnp.zeros_like(dvalues)
    bias = bias_ref[0]
    key_at = lax.broadcasted_iota(jnp.int32, (block, block), 0)
    query_at = lax.broadcasted_iota(jnp.int32, (block, block), 1)
    older = key_at > query_at
    for qi in range(length // block):
        here = slice(qi * block, (qi + 1) * block)
        query = q_ref[0, here]
        grad = g_ref[0, here]
        query_t = query.T
        grad_t = grad.T

        def rows_of(part):
            start = qi * block + part * block
            return slice(start, start + block)

        def is_prior(part):
            return (qi + part) * block < length

        peak = jnp.full((1, block), NEG, F32)
        for part in range(parts):
            score = matmul(keys[rows_of(part)], query_t)
            if part == 0:
                score = jnp.where(older, score, NEG)
            if part == parts - 1:
                score = jnp.where(older, NEG, score)
            top = jnp.max(score, axis=0, keepdims=True)
            if is_prior(part):
                top = top + bias
            peak = jnp.maximum(peak, top)
            scores[part * block : (part + 1) * block] = score
        factor = SCALING * LOG2E
        scaled_peak = peak * factor
        shifted_prior = (peak - bias) * factor
        total = jnp.zeros((1, block), F32)
        for part in range(parts):
            rows = slice(part * block, (part + 1) * block)
            shift = shifted_prior if is_prior(part) else scaled_peak
            weight = jnp.exp2(scores[rows] * factor - shift)
            total = total + jnp.sum(weight, axis=0, keepdims=True)
            scores[rows] = weight
        inverse = 1.0 / total
        attended = jnp.zeros((HDIM, block), F32)
        for part in range(parts):
            rows = slice(part * block, (part + 1) * block)
            weight = scores[rows].astype(BF16)
            attended = attended + matmul(values_t[:, rows_of(part)], weight)
        attended = (attended * inverse).astype(BF16)
        out_ref[0, here] = attended.T
        row_dot = jnp.sum(
            attended.astype(F32) * grad_t.astype(F32), axis=0, keepdims=True
        )
        query_grad = jnp.zeros((HDIM, block), F32)
        for part in range(parts):
            rows = slice(part * block, (part + 1) * block)
            probability = scores[rows] * inverse
            dprob = matmul(values[rows_of(part)], grad_t)
            dscore = (probability * (dprob - row_dot)).astype(BF16)
            query_grad = query_grad + matmul(keys_t[:, rows_of(part)], dscore)
            dkeys[rows_of(part)] += matmul(dscore, query)
            dvalues[rows_of(part)] += matmul(probability.astype(BF16), grad)
        dq_ref[0, here] = (query_grad * SCALING).astype(BF16).T
    dk_ref[0] = (dkeys[length:] * SCALING).astype(BF16)
    dv_ref[0] = dvalues[length:].astype(BF16)
    dk_prior[0] = (dkeys[:length] * SCALING).astype(BF16)
    dv_prior[0] = dvalues[:length].astype(BF16)


def row_heads(piece, bias, arrays, prior, made):
    _, length, width = arrays[0].shape
    block = 256
    window = length + block
    heads = HALF // PIECES
    one = pl.BlockSpec((1, length, HDIM), lambda h: (0, 0, piece * heads + h))
    two = pl.BlockSpec((2, length, HDIM), lambda h: (0, 0, h))
    shape = jax.ShapeDtypeStruct((1, length, width), BF16)
    partial_shape = jax.ShapeDtypeStruct((1, length, HALF * HDIM), BF16)
    return pl.pallas_call(
        functools.partial(row_kernel, block, len(made)),
        grid=(heads,),
        in_specs=[pl.BlockSpec(memory_space=pltpu.SMEM)]
        + [one] * 4
        + [two]
        + [pl.BlockSpec(memory_space=pl.ANY)] * len(made),
        out_specs=[one] * 6,
        out_shape=[shape] * 4 + [partial_shape] * 2,
        input_output_aliases={6 + at: at for at in range(len(made))},
        scratch_shapes=[
            pltpu.VMEM((2 * length, HDIM), BF16),
            pltpu.VMEM((2 * length, HDIM), BF16),
            pltpu.VMEM((HDIM, 2 * length), BF16),
            pltpu.VMEM((HDIM, 2 * length), BF16),
            pltpu.VMEM((window, block), F32),
            pltpu.VMEM((2 * length, HDIM), F32),
            pltpu.VMEM((2 * length, HDIM), F32),
        ],
        compiler_params=params(),
        cost_estimate=pl.CostEstimate(
            flops=AHEAD * heads * length * window * HDIM,
            bytes_accessed=24 * heads * length * HDIM,
            transcendentals=heads * length * window,
        ),
        name="row_heads",
    )(bias, *arrays, prior, *made)


def column_kernel(row_down, row_across, in_ref, out_ref, *scratch):
    rows, _, per, _ = in_ref.shape
    staged, results = scratch[:4], scratch[4:]
    for at, ref in enumerate(staged):
        ref[...] = in_ref[:, at].astype(F32).reshape(rows * per, HDIM)
    causal = row_down[...] <= row_across[...]
    factor = SCALING * LOG2E
    columns = range(per)
    picks = [pl.ds(column, rows, stride=per) for column in columns]
    query, key, value, grad = [
        [ref[pick, :].astype(BF16) for pick in picks] for ref in staged
    ]
    score = [jnp.where(causal, matmul_nt(key[c], query[c]), NEG) for c in columns]
    dprob = [matmul_nt(value[c], grad[c]) for c in columns]
    peak = [jnp.max(score[c], axis=0, keepdims=True) for c in columns]
    weight = [jnp.exp2((score[c] - peak[c]) * factor) for c in columns]
    inverse = [1.0 / jnp.sum(weight[c], axis=0, keepdims=True) for c in columns]
    probability = [weight[c] * inverse[c] for c in columns]
    low = [probability[c].astype(BF16) for c in columns]
    row_dot = [jnp.sum(probability[c] * dprob[c], axis=0, keepdims=True) for c in columns]
    dscore = [(probability[c] * (dprob[c] - row_dot[c])).astype(BF16) for c in columns]
    for c in columns:
        results[0][picks[c], :] = matmul_tn(low[c], value[c])
    for c in columns:
        results[3][picks[c], :] = matmul(low[c], grad[c])
    for c in columns:
        results[1][picks[c], :] = matmul_tn(dscore[c], key[c]) * SCALING
    for c in columns:
        results[2][picks[c], :] = matmul(dscore[c], query[c]) * SCALING
    for at, ref in enumerate(results):
        out_ref[:, at] = ref[...].reshape(rows, per, HDIM).astype(BF16)


def column_heads(arrived, order):
    rows, _, per, half = arrived.shape
    row_ids = jnp.array(order, jnp.int32)
    spec = pl.BlockSpec((rows, 4, per, HDIM), lambda h: (0, 0, 0, h))
    return pl.pallas_call(
        column_kernel,
        grid=(HALF,),
        in_specs=[
            pl.BlockSpec((rows, 1), lambda h: (0, 0)),
            pl.BlockSpec((1, rows), lambda h: (0, 0)),
            spec,
        ],
        out_specs=spec,
        out_shape=jax.ShapeDtypeStruct(arrived.shape, BF16),
        scratch_shapes=[pltpu.VMEM((rows * per, HDIM), F32)] * 8,
        compiler_params=params(),
        cost_estimate=pl.CostEstimate(
            flops=12 * HALF * per * rows * rows * HDIM,
            bytes_accessed=16 * rows * per * half,
            transcendentals=HALF * per * rows * rows,
        ),
        name="column_heads",
    )(row_ids[:, None], row_ids[None, :], arrived)


def add_kernel(dk_back, dv_back, dk_in, dv_in, dk_ref, dv_ref):
    dk_ref[0] = (dk_in[0].astype(F32) + dk_back[0].astype(F32)).astype(BF16)
    dv_ref[0] = (dv_in[0].astype(F32) + dv_back[0].astype(F32)).astype(BF16)


def add_returned(back, row_dk, row_dv):
    _, length, half = back[0].shape
    rows = 512
    left = pl.BlockSpec((1, rows, half), lambda i: (0, i, 0))
    shape = jax.ShapeDtypeStruct(row_dk.shape, BF16)
    return pl.pallas_call(
        add_kernel,
        grid=(length // rows,),
        in_specs=[left] * 4,
        out_specs=[left, left],
        out_shape=[shape] * 2,
        input_output_aliases={2: 0, 3: 1},
        compiler_params=params(),
        cost_estimate=pl.CostEstimate(
            flops=100 * AHEAD * length * HDIM * HDIM,
            bytes_accessed=12 * length * half,
            transcendentals=0,
        ),
        name="add_returned",
    )(*back, row_dk, row_dv)


def place_kernel(cols_ref, *refs):
    outs, (buffer, in_sems, out_sems) = refs[4:8], refs[8:]
    devices, _, per, half = cols_ref.shape
    count = devices // CHUNKS
    moves = []
    for chunk in range(CHUNKS):
        part = pl.ds(chunk * count, count)
        outgoing = [
            (buffer.at[part, at], out.at[part, :, pl.ds(half, half)])
            for at, out in enumerate(outs)
        ]
        moves.append(([(cols_ref.at[part], buffer.at[part])], outgoing))
    stream(moves, in_sems, out_sems)


def place(columns, rowwise):
    devices, _, per, half = columns.shape
    whole = rowwise[0].shape
    shape = (devices, per, whole[2])
    anywhere = pl.BlockSpec(memory_space=pl.ANY)
    placed = pl.pallas_call(
        place_kernel,
        in_specs=[anywhere] * 5,
        out_specs=[anywhere] * 4,
        out_shape=[jax.ShapeDtypeStruct(shape, BF16)] * 4,
        input_output_aliases={1: 0, 2: 1, 3: 2, 4: 3},
        scratch_shapes=[
            pltpu.VMEM(columns.shape, BF16),
            pltpu.SemaphoreType.DMA((CHUNKS, 1)),
            pltpu.SemaphoreType.DMA((CHUNKS, 4)),
        ],
        compiler_params=params(),
        cost_estimate=pl.CostEstimate(
            flops=0, bytes_accessed=16 * devices * per * half, transcendentals=0
        ),
        name="place",
    )(columns, *[array.reshape(shape) for array in rowwise])
    return [array.reshape(whole) for array in placed]


def exchange_order():
    order = []
    for z_hi, z_lo, core, y, x in itertools.product(range(2), range(2), range(2), range(4), range(4)):
        order.append(((z_hi * 4 + y) * 4 + x) * 4 + z_lo * 2 + core)
    return order


def exchange(blocks, order):
    return lax.all_to_all(
        blocks, AXES, split_axis=0, concat_axis=0, axis_index_groups=[order], tiled=True
    )


def on_device(queries, key_vectors, value_vectors, out_cotangent):
    devices = lax.axis_size(AXES)
    order = exchange_order()
    arrays = (queries, key_vectors, value_vectors, out_cotangent)
    forward = [(i, i + 1) for i in range(devices - 1)]
    backward = [(i + 1, i) for i in range(devices - 1)]
    pairs = pack_pairs(key_vectors, value_vectors)
    prior = [lax.ppermute(pair, AXES, forward) for pair in pairs]
    packed = pack_columns(arrays, devices)
    packed, _ = lax.optimization_barrier((packed, prior[0]))
    arrived = exchange(packed, order)
    at_start = lax.axis_index(AXES) == 0
    bias = jnp.where(at_start, NEG, 0.0).astype(F32).reshape(1)
    made = ()
    for piece in range(PIECES):
        made = row_heads(piece, bias, arrays, prior[piece], made)
    row_out, row_dq, row_dk, row_dv, *partials = made
    arrived, *partials = lax.optimization_barrier((arrived, *partials))
    back = [lax.ppermute(partial, AXES, backward) for partial in partials]
    leaving = column_heads(arrived, order)
    leaving, _ = lax.optimization_barrier((leaving, back[0]))
    returned = exchange(leaving, order)
    row_dk, row_dv = add_returned(back, row_dk, row_dv)
    return tuple(place(returned, (row_out, row_dq, row_dk, row_dv)))


def solution(mesh):
    spec = P(AXES, None, None)
    return jax.shard_map(
        on_device, mesh=mesh, in_specs=(spec,) * 4, out_specs=(spec,) * 4, check_vma=False
    )
```

```python
import functools
import itertools
import math

import jax
import jax.numpy as jnp
from jax import lax
from jax.experimental import pallas as pl
from jax.experimental.pallas import tpu as pltpu
from jax.sharding import PartitionSpec as P

HEADS = 8
HDIM = 128
HALF = HEADS // 2
SCALING = HDIM ** (-0.5)
LOG2E = math.log2(math.e)
NEG = -1e30
AHEAD = 1000
PIECES = 2
CHUNKS = 4
VMEM_BYTES = 64 * 1024 * 1024 - 256 * 1024
AXES = ("grp", "seq")
F32 = jnp.float32
BF16 = jnp.bfloat16


def matmul(lhs, rhs):
    return jnp.dot(lhs, rhs, preferred_element_type=F32)


def matmul_nt(lhs, rhs):
    return lax.dot_general(lhs, rhs, (((1,), (1,)), ((), ())), preferred_element_type=F32)


def matmul_tn(lhs, rhs):
    return lax.dot_general(lhs, rhs, (((0,), (0,)), ((), ())), preferred_element_type=F32)


def params():
    return pltpu.CompilerParams(vmem_limit_bytes=VMEM_BYTES)


def stream(moves, in_sems, out_sems):
    arriving = []
    for incoming, _ in moves:
        started = []
        for source, target in incoming:
            started.append(pltpu.make_async_copy(source, target, in_sems.at[len(arriving), len(started)]))
            started[-1].start()
        arriving.append(started)
    leaving = []
    for at, (_, outgoing) in enumerate(moves):
        for copy in arriving[at]:
            copy.wait()
        for source, target in outgoing:
            copy = pltpu.make_async_copy(source, target, out_sems.at[at, len(leaving) % len(outgoing)])
            copy.start()
            leaving.append(copy)
    for copy in leaving:
        copy.wait()


def pair_kernel(first, k_ref, v_ref, out_ref, buffer, in_sems, out_sems):
    here = pl.ds(first, out_ref.shape[2])
    moves = [
        ([(ref.at[0, :, here], buffer.at[at])], [(buffer.at[at], out_ref.at[at])])
        for at, ref in enumerate((k_ref, v_ref))
    ]
    stream(moves, in_sems, out_sems)


def pack_pair(key_vectors, value_vectors, piece):
    _, length, width = key_vectors.shape
    wide = width // 2 // PIECES
    anywhere = pl.BlockSpec(memory_space=pl.ANY)
    return pl.pallas_call(
        functools.partial(pair_kernel, piece * wide),
        in_specs=[anywhere] * 2,
        out_specs=anywhere,
        out_shape=jax.ShapeDtypeStruct((2, length, wide), BF16),
        scratch_shapes=[
            pltpu.VMEM((2, length, wide), BF16),
            pltpu.SemaphoreType.DMA((2, 1)),
            pltpu.SemaphoreType.DMA((2, 1)),
        ],
        compiler_params=params(),
        cost_estimate=pl.CostEstimate(
            flops=0, bytes_accessed=8 * length * wide, transcendentals=0
        ),
        name="pack_pair",
    )(key_vectors, value_vectors)


def pack_kernel(q_ref, k_ref, v_ref, g_ref, out_ref, buffer, in_sems, out_sems):
    devices, _, per, half = out_ref.shape
    count = devices // CHUNKS
    moves = []
    for chunk in range(CHUNKS):
        part = pl.ds(chunk * count, count)
        incoming = [
            (ref.at[part, :, pl.ds(half, half)], buffer.at[part, at])
            for at, ref in enumerate((q_ref, k_ref, v_ref, g_ref))
        ]
        moves.append((incoming, [(buffer.at[part], out_ref.at[part])]))
    stream(moves, in_sems, out_sems)


def pack_columns(arrays, devices):
    _, length, width = arrays[0].shape
    half = width // 2
    per = length // devices
    anywhere = pl.BlockSpec(memory_space=pl.ANY)
    shape = (devices, 4, per, half)
    return pl.pallas_call(
        pack_kernel,
        in_specs=[anywhere] * 4,
        out_specs=anywhere,
        out_shape=jax.ShapeDtypeStruct(shape, BF16),
        scratch_shapes=[
            pltpu.VMEM(shape, BF16),
            pltpu.SemaphoreType.DMA((CHUNKS, 4)),
            pltpu.SemaphoreType.DMA((CHUNKS, 1)),
        ],
        compiler_params=params(),
        cost_estimate=pl.CostEstimate(
            flops=0, bytes_accessed=16 * length * half, transcendentals=0
        ),
        name="pack_columns",
    )(*[array.reshape(devices, per, width) for array in arrays])


def row_kernel(block, made, bias_ref, q_ref, k_ref, v_ref, g_ref, prior_ref, *refs):
    out_ref, dq_ref, dk_ref, dv_ref, dk_prior, dv_prior = refs[made : made + 6]
    keys, values, keys_t, values_t, scores, dkeys, dvalues = refs[made + 6 :]
    length = q_ref.shape[1]
    window = length + block
    parts = window // block
    keys[:length] = prior_ref[0]
    keys[length:] = k_ref[0]
    values[:length] = prior_ref[1]
    values[length:] = v_ref[0]
    for at in range(0, 2 * length, block):
        rows = slice(at, at + block)
        keys_t[:, rows] = keys[rows].T
        values_t[:, rows] = values[rows].T
    dkeys[...] = jnp.zeros_like(dkeys)
    dvalues[...] = jnp.zeros_like(dvalues)
    bias = bias_ref[0]
    key_at = lax.broadcasted_iota(jnp.int32, (block, block), 0)
    query_at = lax.broadcasted_iota(jnp.int32, (block, block), 1)
    older = key_at > query_at
    for qi in range(length // block):
        here = slice(qi * block, (qi + 1) * block)
        query = q_ref[0, here]
        grad = g_ref[0, here]
        query_t = query.T
        grad_t = grad.T

        def rows_of(part):
            start = qi * block + part * block
            return slice(start, start + block)

        def is_prior(part):
            return (qi + part) * block < length

        peak = jnp.full((1, block), NEG, F32)
        for part in range(parts):
            score = matmul(keys[rows_of(part)], query_t)
            if part == 0:
                score = jnp.where(older, score, NEG)
            if part == parts - 1:
                score = jnp.where(older, NEG, score)
            top = jnp.max(score, axis=0, keepdims=True)
            if is_prior(part):
                top = top + bias
            peak = jnp.maximum(peak, top)
            scores[part * block : (part + 1) * block] = score
        factor = SCALING * LOG2E
        scaled_peak = peak * factor
        shifted_prior = (peak - bias) * factor
        total = jnp.zeros((1, block), F32)
        for part in range(parts):
            rows = slice(part * block, (part + 1) * block)
            shift = shifted_prior if is_prior(part) else scaled_peak
            weight = jnp.exp2(scores[rows] * factor - shift)
            total = total + jnp.sum(weight, axis=0, keepdims=True)
            scores[rows] = weight
        inverse = 1.0 / total
        attended = jnp.zeros((HDIM, block), F32)
        for part in range(parts):
            rows = slice(part * block, (part + 1) * block)
            weight = scores[rows].astype(BF16)
            attended = attended + matmul(values_t[:, rows_of(part)], weight)
        attended = (attended * inverse).astype(BF16)
        out_ref[0, here] = attended.T
        row_dot = jnp.sum(
            attended.astype(F32) * grad_t.astype(F32), axis=0, keepdims=True
        )
        query_grad = jnp.zeros((HDIM, block), F32)
        for part in range(parts):
            rows = slice(part * block, (part + 1) * block)
            probability = scores[rows] * inverse
            dprob = matmul(values[rows_of(part)], grad_t)
            dscore = (probability * (dprob - row_dot)).astype(BF16)
            query_grad = query_grad + matmul(keys_t[:, rows_of(part)], dscore)
            dkeys[rows_of(part)] += matmul(dscore, query)
            dvalues[rows_of(part)] += matmul(probability.astype(BF16), grad)
        dq_ref[0, here] = (query_grad * SCALING).astype(BF16).T
    dk_ref[0] = (dkeys[length:] * SCALING).astype(BF16)
    dv_ref[0] = dvalues[length:].astype(BF16)
    dk_prior[0] = (dkeys[:length] * SCALING).astype(BF16)
    dv_prior[0] = dvalues[:length].astype(BF16)


def row_heads(piece, bias, arrays, prior, made):
    _, length, width = arrays[0].shape
    block = 256
    window = length + block
    heads = HALF // PIECES
    one = pl.BlockSpec((1, length, HDIM), lambda h: (0, 0, piece * heads + h))
    two = pl.BlockSpec((2, length, HDIM), lambda h: (0, 0, h))
    shape = jax.ShapeDtypeStruct((1, length, width), BF16)
    partial_shape = jax.ShapeDtypeStruct((1, length, HALF * HDIM), BF16)
    return pl.pallas_call(
        functools.partial(row_kernel, block, len(made)),
        grid=(heads,),
        in_specs=[pl.BlockSpec(memory_space=pltpu.SMEM)]
        + [one] * 4
        + [two]
        + [pl.BlockSpec(memory_space=pl.ANY)] * len(made),
        out_specs=[one] * 6,
        out_shape=[shape] * 4 + [partial_shape] * 2,
        input_output_aliases={6 + at: at for at in range(len(made))},
        scratch_shapes=[
            pltpu.VMEM((2 * length, HDIM), BF16),
            pltpu.VMEM((2 * length, HDIM), BF16),
            pltpu.VMEM((HDIM, 2 * length), BF16),
            pltpu.VMEM((HDIM, 2 * length), BF16),
            pltpu.VMEM((window, block), F32),
            pltpu.VMEM((2 * length, HDIM), F32),
            pltpu.VMEM((2 * length, HDIM), F32),
        ],
        compiler_params=params(),
        cost_estimate=pl.CostEstimate(
            flops=AHEAD * heads * length * window * HDIM,
            bytes_accessed=24 * heads * length * HDIM,
            transcendentals=heads * length * window,
        ),
        name="row_heads",
    )(bias, *arrays, prior, *made)


def column_kernel(row_down, row_across, in_ref, out_ref, *scratch):
    rows, _, per, _ = in_ref.shape
    staged, results = scratch[:4], scratch[4:]
    for at, ref in enumerate(staged):
        ref[: rows * per] = in_ref[:, at].astype(F32).reshape(rows * per, HDIM)
    causal = row_down[...] <= row_across[...]
    factor = SCALING * LOG2E
    columns = range(per)
    picks = [pl.ds(column, rows, stride=per) for column in columns]
    query, key, value, grad = [
        [ref[pick, :].astype(BF16) for pick in picks] for ref in staged
    ]
    score = [jnp.where(causal, matmul_nt(key[c], query[c]), NEG) for c in columns]
    dprob = [matmul_nt(value[c], grad[c]) for c in columns]
    peak = [jnp.max(score[c], axis=0, keepdims=True) for c in columns]
    weight = [jnp.exp2((score[c] - peak[c]) * factor) for c in columns]
    inverse = [1.0 / jnp.sum(weight[c], axis=0, keepdims=True) for c in columns]
    probability = [weight[c] * inverse[c] for c in columns]
    low = [probability[c].astype(BF16) for c in columns]
    row_dot = [jnp.sum(probability[c] * dprob[c], axis=0, keepdims=True) for c in columns]
    dscore = [(probability[c] * (dprob[c] - row_dot[c])).astype(BF16) for c in columns]
    for c in columns:
        results[0][picks[c], :] = matmul_tn(low[c], value[c])
    for c in columns:
        results[3][picks[c], :] = matmul(low[c], grad[c])
    for c in columns:
        results[1][picks[c], :] = matmul_tn(dscore[c], key[c]) * SCALING
    for c in columns:
        results[2][picks[c], :] = matmul(dscore[c], query[c]) * SCALING
    for at, ref in enumerate(results):
        out_ref[:, at] = ref[: rows * per].reshape(rows, per, HDIM).astype(BF16)


def column_heads(arrived, order):
    rows, _, per, half = arrived.shape
    row_ids = jnp.array(order, jnp.int32)
    spec = pl.BlockSpec((rows, 4, per, HDIM), lambda h: (0, 0, 0, h))
    return pl.pallas_call(
        column_kernel,
        grid=(HALF,),
        in_specs=[
            pl.BlockSpec((rows, 1), lambda h: (0, 0)),
            pl.BlockSpec((1, rows), lambda h: (0, 0)),
            spec,
        ],
        out_specs=spec,
        out_shape=jax.ShapeDtypeStruct(arrived.shape, BF16),
        scratch_shapes=[pltpu.VMEM((rows * per + per, HDIM), F32)] * 8,
        compiler_params=params(),
        cost_estimate=pl.CostEstimate(
            flops=12 * HALF * per * rows * rows * HDIM,
            bytes_accessed=16 * rows * per * half,
            transcendentals=HALF * per * rows * rows,
        ),
        name="column_heads",
    )(row_ids[:, None], row_ids[None, :], arrived)


def add_kernel(dk_back, dv_back, dk_in, dv_in, dk_ref, dv_ref):
    dk_ref[0] = (dk_in[0].astype(F32) + dk_back[0].astype(F32)).astype(BF16)
    dv_ref[0] = (dv_in[0].astype(F32) + dv_back[0].astype(F32)).astype(BF16)


def add_returned(back, row_dk, row_dv):
    _, length, half = back[0].shape
    rows = 512
    left = pl.BlockSpec((1, rows, half), lambda i: (0, i, 0))
    shape = jax.ShapeDtypeStruct(row_dk.shape, BF16)
    return pl.pallas_call(
        add_kernel,
        grid=(length // rows,),
        in_specs=[left] * 4,
        out_specs=[left, left],
        out_shape=[shape] * 2,
        input_output_aliases={2: 0, 3: 1},
        compiler_params=params(),
        cost_estimate=pl.CostEstimate(
            flops=100 * AHEAD * length * HDIM * HDIM,
            bytes_accessed=12 * length * half,
            transcendentals=0,
        ),
        name="add_returned",
    )(*back, row_dk, row_dv)


def place_kernel(cols_ref, *refs):
    outs, (buffer, in_sems, out_sems) = refs[4:8], refs[8:]
    devices, _, per, half = cols_ref.shape
    count = devices // CHUNKS
    moves = []
    for chunk in range(CHUNKS):
        part = pl.ds(chunk * count, count)
        outgoing = [
            (buffer.at[part, at], out.at[part, :, pl.ds(half, half)])
            for at, out in enumerate(outs)
        ]
        moves.append(([(cols_ref.at[part], buffer.at[part])], outgoing))
    stream(moves, in_sems, out_sems)


def place(columns, rowwise):
    devices, _, per, half = columns.shape
    whole = rowwise[0].shape
    shape = (devices, per, whole[2])
    anywhere = pl.BlockSpec(memory_space=pl.ANY)
    placed = pl.pallas_call(
        place_kernel,
        in_specs=[anywhere] * 5,
        out_specs=[anywhere] * 4,
        out_shape=[jax.ShapeDtypeStruct(shape, BF16)] * 4,
        input_output_aliases={1: 0, 2: 1, 3: 2, 4: 3},
        scratch_shapes=[
            pltpu.VMEM(columns.shape, BF16),
            pltpu.SemaphoreType.DMA((CHUNKS, 1)),
            pltpu.SemaphoreType.DMA((CHUNKS, 4)),
        ],
        compiler_params=params(),
        cost_estimate=pl.CostEstimate(
            flops=0, bytes_accessed=16 * devices * per * half, transcendentals=0
        ),
        name="place",
    )(columns, *[array.reshape(shape) for array in rowwise])
    return [array.reshape(whole) for array in placed]


def exchange_order():
    order = []
    for z_hi, z_lo, core, y, x in itertools.product(range(2), range(2), range(2), range(4), range(4)):
        order.append(((z_hi * 4 + y) * 4 + x) * 4 + z_lo * 2 + core)
    return order


def exchange(blocks, order):
    return lax.all_to_all(
        blocks, AXES, split_axis=0, concat_axis=0, axis_index_groups=[order], tiled=True
    )


def on_device(queries, key_vectors, value_vectors, out_cotangent):
    devices = lax.axis_size(AXES)
    order = exchange_order()
    arrays = (queries, key_vectors, value_vectors, out_cotangent)
    forward = [(i, i + 1) for i in range(devices - 1)]
    backward = [(i + 1, i) for i in range(devices - 1)]
    prior, pair = [], None
    for piece in range(PIECES):
        sources = (key_vectors, value_vectors)
        if pair is not None:
            *sources, _ = lax.optimization_barrier((*sources, pair))
        pair = pack_pair(*sources, piece)
        prior.append(lax.ppermute(pair, AXES, forward))
    packed = pack_columns(arrays, devices)
    packed, _ = lax.optimization_barrier((packed, prior[0]))
    arrived = exchange(packed, order)
    at_start = lax.axis_index(AXES) == 0
    bias = jnp.where(at_start, NEG, 0.0).astype(F32).reshape(1)
    made = ()
    for piece in range(PIECES):
        made = row_heads(piece, bias, arrays, prior[piece], made)
    row_out, row_dq, row_dk, row_dv, *partials = made
    arrived, *partials = lax.optimization_barrier((arrived, *partials))
    back = [lax.ppermute(partial, AXES, backward) for partial in partials]
    leaving = column_heads(arrived, order)
    leaving, _ = lax.optimization_barrier((leaving, back[0]))
    returned = exchange(leaving, order)
    row_dk, row_dv = add_returned(back, row_dk, row_dv)
    return tuple(place(returned, (row_out, row_dq, row_dk, row_dv)))


def solution(mesh):
    spec = P(AXES, None, None)
    return jax.shard_map(
        on_device, mesh=mesh, in_specs=(spec,) * 4, out_specs=(spec,) * 4, check_vma=False
    )
```

```python
import functools
import itertools
import math

import jax
import jax.numpy as jnp
from jax import lax
from jax.experimental import pallas as pl
from jax.experimental.pallas import tpu as pltpu
from jax.sharding import PartitionSpec as P

HEADS = 8
HDIM = 128
HALF = HEADS // 2
SCALING = HDIM ** (-0.5)
LOG2E = math.log2(math.e)
NEG = -1e30
AHEAD = 1000
PIECES = 2
CHUNKS = 4
VMEM_BYTES = 64 * 1024 * 1024 - 256 * 1024
AXES = ("grp", "seq")
F32 = jnp.float32
BF16 = jnp.bfloat16


def matmul(lhs, rhs):
    return jnp.dot(lhs, rhs, preferred_element_type=F32)


def matmul_nt(lhs, rhs):
    return lax.dot_general(lhs, rhs, (((1,), (1,)), ((), ())), preferred_element_type=F32)


def matmul_tn(lhs, rhs):
    return lax.dot_general(lhs, rhs, (((0,), (0,)), ((), ())), preferred_element_type=F32)


def params():
    return pltpu.CompilerParams(vmem_limit_bytes=VMEM_BYTES)


def stream(moves, in_sems, out_sems):
    arriving = []
    for incoming, _ in moves:
        started = []
        for source, target in incoming:
            started.append(pltpu.make_async_copy(source, target, in_sems.at[len(arriving), len(started)]))
            started[-1].start()
        arriving.append(started)
    leaving = []
    for at, (_, outgoing) in enumerate(moves):
        for copy in arriving[at]:
            copy.wait()
        for source, target in outgoing:
            copy = pltpu.make_async_copy(source, target, out_sems.at[at, len(leaving) % len(outgoing)])
            copy.start()
            leaving.append(copy)
    for copy in leaving:
        copy.wait()


def pair_kernel(first, k_ref, v_ref, out_ref, buffer, in_sems, out_sems):
    here = pl.ds(first, out_ref.shape[2])
    moves = [
        ([(ref.at[0, :, here], buffer.at[at])], [(buffer.at[at], out_ref.at[at])])
        for at, ref in enumerate((k_ref, v_ref))
    ]
    stream(moves, in_sems, out_sems)


def pack_pair(key_vectors, value_vectors, piece):
    _, length, width = key_vectors.shape
    wide = width // 2 // PIECES
    anywhere = pl.BlockSpec(memory_space=pl.ANY)
    return pl.pallas_call(
        functools.partial(pair_kernel, piece * wide),
        in_specs=[anywhere] * 2,
        out_specs=anywhere,
        out_shape=jax.ShapeDtypeStruct((2, length, wide), BF16),
        scratch_shapes=[
            pltpu.VMEM((2, length, wide), BF16),
            pltpu.SemaphoreType.DMA((2, 1)),
            pltpu.SemaphoreType.DMA((2, 1)),
        ],
        compiler_params=params(),
        cost_estimate=pl.CostEstimate(
            flops=0, bytes_accessed=8 * length * wide, transcendentals=0
        ),
        name="pack_pair",
    )(key_vectors, value_vectors)


def pack_kernel(q_ref, k_ref, v_ref, g_ref, out_ref, buffer, in_sems, out_sems):
    devices, _, per, half = out_ref.shape
    count = devices // CHUNKS
    moves = []
    for chunk in range(CHUNKS):
        part = pl.ds(chunk * count, count)
        incoming = [
            (ref.at[part, :, pl.ds(half, half)], buffer.at[part, at])
            for at, ref in enumerate((q_ref, k_ref, v_ref, g_ref))
        ]
        moves.append((incoming, [(buffer.at[part], out_ref.at[part])]))
    stream(moves, in_sems, out_sems)


def pack_columns(arrays, devices):
    _, length, width = arrays[0].shape
    half = width // 2
    per = length // devices
    anywhere = pl.BlockSpec(memory_space=pl.ANY)
    shape = (devices, 4, per, half)
    return pl.pallas_call(
        pack_kernel,
        in_specs=[anywhere] * 4,
        out_specs=anywhere,
        out_shape=jax.ShapeDtypeStruct(shape, BF16),
        scratch_shapes=[
            pltpu.VMEM(shape, BF16),
            pltpu.SemaphoreType.DMA((CHUNKS, 4)),
            pltpu.SemaphoreType.DMA((CHUNKS, 1)),
        ],
        compiler_params=params(),
        cost_estimate=pl.CostEstimate(
            flops=0, bytes_accessed=16 * length * half, transcendentals=0
        ),
        name="pack_columns",
    )(*[array.reshape(devices, per, width) for array in arrays])


def row_kernel(block, made, bias_ref, q_ref, k_ref, v_ref, g_ref, prior_ref, *refs):
    out_ref, dq_ref, dk_ref, dv_ref, dk_prior, dv_prior = refs[made : made + 6]
    keys, values, keys_t, values_t, scores, dkeys, dvalues = refs[made + 6 :]
    length = q_ref.shape[1]
    window = length + block
    parts = window // block
    keys[:length] = prior_ref[0]
    keys[length:] = k_ref[0]
    values[:length] = prior_ref[1]
    values[length:] = v_ref[0]
    for at in range(0, 2 * length, block):
        rows = slice(at, at + block)
        keys_t[:, rows] = keys[rows].T
        values_t[:, rows] = values[rows].T
    dkeys[...] = jnp.zeros_like(dkeys)
    dvalues[...] = jnp.zeros_like(dvalues)
    bias = bias_ref[0]
    key_at = lax.broadcasted_iota(jnp.int32, (block, block), 0)
    query_at = lax.broadcasted_iota(jnp.int32, (block, block), 1)
    older = key_at > query_at
    for qi in range(length // block):
        here = slice(qi * block, (qi + 1) * block)
        query = q_ref[0, here]
        grad = g_ref[0, here]
        query_t = query.T
        grad_t = grad.T

        def rows_of(part):
            start = qi * block + part * block
            return slice(start, start + block)

        def is_prior(part):
            return (qi + part) * block < length

        peak = jnp.full((1, block), NEG, F32)
        for part in range(parts):
            score = matmul(keys[rows_of(part)], query_t)
            if part == 0:
                score = jnp.where(older, score, NEG)
            if part == parts - 1:
                score = jnp.where(older, NEG, score)
            top = jnp.max(score, axis=0, keepdims=True)
            if is_prior(part):
                top = top + bias
            peak = jnp.maximum(peak, top)
            scores[part * block : (part + 1) * block] = score
        factor = SCALING * LOG2E
        scaled_peak = peak * factor
        shifted_prior = (peak - bias) * factor
        total = jnp.zeros((1, block), F32)
        for part in range(parts):
            rows = slice(part * block, (part + 1) * block)
            shift = shifted_prior if is_prior(part) else scaled_peak
            weight = jnp.exp2(scores[rows] * factor - shift)
            total = total + jnp.sum(weight, axis=0, keepdims=True)
            scores[rows] = weight
        inverse = 1.0 / total
        attended = jnp.zeros((HDIM, block), F32)
        for part in range(parts):
            rows = slice(part * block, (part + 1) * block)
            weight = scores[rows].astype(BF16)
            attended = attended + matmul(values_t[:, rows_of(part)], weight)
        attended = (attended * inverse).astype(BF16)
        out_ref[0, here] = attended.T
        row_dot = jnp.sum(
            attended.astype(F32) * grad_t.astype(F32), axis=0, keepdims=True
        )
        query_grad = jnp.zeros((HDIM, block), F32)
        for part in range(parts):
            rows = slice(part * block, (part + 1) * block)
            probability = scores[rows] * inverse
            dprob = matmul(values[rows_of(part)], grad_t)
            dscore = (probability * (dprob - row_dot)).astype(BF16)
            query_grad = query_grad + matmul(keys_t[:, rows_of(part)], dscore)
            dkeys[rows_of(part)] += matmul(dscore, query)
            dvalues[rows_of(part)] += matmul(probability.astype(BF16), grad)
        dq_ref[0, here] = (query_grad * SCALING).astype(BF16).T
    dk_ref[0] = (dkeys[length:] * SCALING).astype(BF16)
    dv_ref[0] = dvalues[length:].astype(BF16)
    dk_prior[0] = (dkeys[:length] * SCALING).astype(BF16)
    dv_prior[0] = dvalues[:length].astype(BF16)


def row_heads(piece, bias, arrays, prior, made):
    _, length, width = arrays[0].shape
    block = 256
    window = length + block
    heads = HALF // PIECES
    one = pl.BlockSpec((1, length, HDIM), lambda h: (0, 0, piece * heads + h))
    two = pl.BlockSpec((2, length, HDIM), lambda h: (0, 0, h))
    shape = jax.ShapeDtypeStruct((1, length, width), BF16)
    partial_shape = jax.ShapeDtypeStruct((1, length, HALF * HDIM), BF16)
    return pl.pallas_call(
        functools.partial(row_kernel, block, len(made)),
        grid=(heads,),
        in_specs=[pl.BlockSpec(memory_space=pltpu.SMEM)]
        + [one] * 4
        + [two]
        + [pl.BlockSpec(memory_space=pl.ANY)] * len(made),
        out_specs=[one] * 6,
        out_shape=[shape] * 4 + [partial_shape] * 2,
        input_output_aliases={6 + at: at for at in range(len(made))},
        scratch_shapes=[
            pltpu.VMEM((2 * length, HDIM), BF16),
            pltpu.VMEM((2 * length, HDIM), BF16),
            pltpu.VMEM((HDIM, 2 * length), BF16),
            pltpu.VMEM((HDIM, 2 * length), BF16),
            pltpu.VMEM((window, block), F32),
            pltpu.VMEM((2 * length, HDIM), F32),
            pltpu.VMEM((2 * length, HDIM), F32),
        ],
        compiler_params=params(),
        cost_estimate=pl.CostEstimate(
            flops=AHEAD * heads * length * window * HDIM,
            bytes_accessed=24 * heads * length * HDIM,
            transcendentals=heads * length * window,
        ),
        name="row_heads",
    )(bias, *arrays, prior, *made)


def column_kernel(row_down, row_across, in_ref, out_ref, *scratch):
    rows, _, per, _ = in_ref.shape
    staged, results = scratch[:4], scratch[4:]
    for at, ref in enumerate(staged):
        ref[: rows * per] = in_ref[:, at].astype(F32).reshape(rows * per, HDIM)
    causal = row_down[...] <= row_across[...]
    factor = SCALING * LOG2E
    columns = range(per)
    picks = [pl.ds(column, rows, stride=per) for column in columns]
    query, key, value, grad = [
        [ref[pick, :].astype(BF16) for pick in picks] for ref in staged
    ]
    score = [jnp.where(causal, matmul_nt(key[c], query[c]), NEG) for c in columns]
    dprob = [matmul_nt(value[c], grad[c]) for c in columns]
    peak = [jnp.max(score[c], axis=0, keepdims=True) for c in columns]
    weight = [jnp.exp2((score[c] - peak[c]) * factor) for c in columns]
    inverse = [1.0 / jnp.sum(weight[c], axis=0, keepdims=True) for c in columns]
    probability = [weight[c] * inverse[c] for c in columns]
    low = [probability[c].astype(BF16) for c in columns]
    row_dot = [jnp.sum(probability[c] * dprob[c], axis=0, keepdims=True) for c in columns]
    dscore = [(probability[c] * (dprob[c] - row_dot[c])).astype(BF16) for c in columns]
    for c in columns:
        results[0][picks[c], :] = matmul_tn(low[c], value[c])
    for c in columns:
        results[3][picks[c], :] = matmul(low[c], grad[c])
    for c in columns:
        results[1][picks[c], :] = matmul_tn(dscore[c], key[c]) * SCALING
    for c in columns:
        results[2][picks[c], :] = matmul(dscore[c], query[c]) * SCALING
    for at, ref in enumerate(results):
        out_ref[:, at] = ref[: rows * per].reshape(rows, per, HDIM).astype(BF16)


def column_heads(arrived, order):
    rows, _, per, half = arrived.shape
    row_ids = jnp.array(order, jnp.int32)
    spec = pl.BlockSpec((rows, 4, per, HDIM), lambda h: (0, 0, 0, h))
    return pl.pallas_call(
        column_kernel,
        grid=(HALF,),
        in_specs=[
            pl.BlockSpec((rows, 1), lambda h: (0, 0)),
            pl.BlockSpec((1, rows), lambda h: (0, 0)),
            spec,
        ],
        out_specs=spec,
        out_shape=jax.ShapeDtypeStruct(arrived.shape, BF16),
        scratch_shapes=[pltpu.VMEM((rows * per + per, HDIM), F32)] * 8,
        compiler_params=params(),
        cost_estimate=pl.CostEstimate(
            flops=12 * HALF * per * rows * rows * HDIM,
            bytes_accessed=16 * rows * per * half,
            transcendentals=HALF * per * rows * rows,
        ),
        name="column_heads",
    )(row_ids[:, None], row_ids[None, :], arrived)


def add_kernel(dk_back, dv_back, dk_in, dv_in, dk_ref, dv_ref):
    dk_ref[0] = (dk_in[0].astype(F32) + dk_back[0].astype(F32)).astype(BF16)
    dv_ref[0] = (dv_in[0].astype(F32) + dv_back[0].astype(F32)).astype(BF16)


def add_returned(back, row_dk, row_dv):
    _, length, half = back[0].shape
    rows = 512
    left = pl.BlockSpec((1, rows, half), lambda i: (0, i, 0))
    shape = jax.ShapeDtypeStruct(row_dk.shape, BF16)
    return pl.pallas_call(
        add_kernel,
        grid=(length // rows,),
        in_specs=[left] * 4,
        out_specs=[left, left],
        out_shape=[shape] * 2,
        input_output_aliases={2: 0, 3: 1},
        compiler_params=params(),
        cost_estimate=pl.CostEstimate(
            flops=100 * AHEAD * length * HDIM * HDIM,
            bytes_accessed=12 * length * half,
            transcendentals=0,
        ),
        name="add_returned",
    )(*back, row_dk, row_dv)


def place_kernel(cols_ref, *refs):
    outs, (buffer, in_sems, out_sems) = refs[4:8], refs[8:]
    devices, _, per, half = cols_ref.shape
    count = devices // CHUNKS
    moves = []
    for chunk in range(CHUNKS):
        part = pl.ds(chunk * count, count)
        outgoing = [
            (buffer.at[part, at], out.at[part, :, pl.ds(half, half)])
            for at, out in enumerate(outs)
        ]
        moves.append(([(cols_ref.at[part], buffer.at[part])], outgoing))
    stream(moves, in_sems, out_sems)


def place(columns, rowwise):
    devices, _, per, half = columns.shape
    whole = rowwise[0].shape
    shape = (devices, per, whole[2])
    anywhere = pl.BlockSpec(memory_space=pl.ANY)
    placed = pl.pallas_call(
        place_kernel,
        in_specs=[anywhere] * 5,
        out_specs=[anywhere] * 4,
        out_shape=[jax.ShapeDtypeStruct(shape, BF16)] * 4,
        input_output_aliases={1: 0, 2: 1, 3: 2, 4: 3},
        scratch_shapes=[
            pltpu.VMEM(columns.shape, BF16),
            pltpu.SemaphoreType.DMA((CHUNKS, 1)),
            pltpu.SemaphoreType.DMA((CHUNKS, 4)),
        ],
        compiler_params=params(),
        cost_estimate=pl.CostEstimate(
            flops=0, bytes_accessed=16 * devices * per * half, transcendentals=0
        ),
        name="place",
    )(columns, *[array.reshape(shape) for array in rowwise])
    return [array.reshape(whole) for array in placed]


def exchange_order():
    order = []
    for z_hi, core, z_lo, y, x in itertools.product(range(2), range(2), range(2), range(4), range(4)):
        order.append(((z_hi * 4 + y) * 4 + x) * 4 + z_lo * 2 + core)
    return order


def exchange(blocks, order):
    return lax.all_to_all(
        blocks, AXES, split_axis=0, concat_axis=0, axis_index_groups=[order], tiled=True
    )


def on_device(queries, key_vectors, value_vectors, out_cotangent):
    devices = lax.axis_size(AXES)
    order = exchange_order()
    arrays = (queries, key_vectors, value_vectors, out_cotangent)
    forward = [(i, i + 1) for i in range(devices - 1)]
    backward = [(i + 1, i) for i in range(devices - 1)]
    prior, pair = [], None
    for piece in range(PIECES):
        sources = (key_vectors, value_vectors)
        if pair is not None:
            *sources, _ = lax.optimization_barrier((*sources, pair))
        pair = pack_pair(*sources, piece)
        prior.append(lax.ppermute(pair, AXES, forward))
    packed = pack_columns(arrays, devices)
    packed, _ = lax.optimization_barrier((packed, prior[0]))
    arrived = exchange(packed, order)
    at_start = lax.axis_index(AXES) == 0
    bias = jnp.where(at_start, NEG, 0.0).astype(F32).reshape(1)
    made = ()
    for piece in range(PIECES):
        made = row_heads(piece, bias, arrays, prior[piece], made)
    row_out, row_dq, row_dk, row_dv, *partials = made
    arrived, *partials = lax.optimization_barrier((arrived, *partials))
    back = [lax.ppermute(partial, AXES, backward) for partial in partials]
    leaving = column_heads(arrived, order)
    leaving, _ = lax.optimization_barrier((leaving, back[0]))
    returned = exchange(leaving, order)
    row_dk, row_dv = add_returned(back, row_dk, row_dv)
    return tuple(place(returned, (row_out, row_dq, row_dk, row_dv)))


def solution(mesh):
    spec = P(AXES, None, None)
    return jax.shard_map(
        on_device, mesh=mesh, in_specs=(spec,) * 4, out_specs=(spec,) * 4, check_vma=False
    )
```
